32 devices in a mesh: virt: 8 (over y, x, core), pair: 4 (over z).
Axes of the slice: x: 2, y: 2, z: 4, core: 2. Of those that a mesh axis runs over, the one named last changes fastest.
Arguments:
- lambda_amps: bfloat16 [160, 896, 896], P('pair', 'virt'), may hold values from -0.0234375 to 0.0234375
- t2_amps: bfloat16 [160, 896, 896], P('pair', 'virt'), may hold values from -6 to 6
- chol_ov: bfloat16 [4096, 4, 896], P('pair', None, 'virt'), may hold values from -0.1875 to 0.1875
Outputs:
- density: bfloat16 [4096, 4, 896], P('pair', None, 'virt')
The draws below stay inside these ranges and needn't reach their ends.
All inputs are finite; a program needn't handle non-finite values.
Results may differ from the reference program's by a relative error of at most 0.0049.
Values may be sent and summed in bfloat16 or wider, within the bound.
No kernel may reach another device: no remote copies, remote signals or barrier semaphores. Data moves between devices by JAX's collectives and lax.ppermute only.
A program may use at most 64 MiB of HBM per device.

```python
import jax
import jax.numpy as jnp
from jax import lax

NV = 896
NAUX = 4096
OCC = 4
NPAIR = 160


def spiked(array, key, source, target, parts, factor):
    owner, partner = [(jnp.arange(array.shape[dim]) // (array.shape[dim] // parts)).reshape([-1 if axis == dim else 1 for axis in range(array.ndim)]) for dim in (source, target)]
    chosen = jax.random.permutation(key, parts)[partner]
    strong = (owner == chosen) | (owner == (partner + parts // 2) % parts)
    return jnp.where(strong, factor * array, array)


def levels(own_key, shape, split, smallest, top_value):
    loudness, own = 1.0, jax.random.fold_in(own_key, 6)
    for dim, blocks in split:
        steps = jnp.exp(jax.random.uniform(jax.random.fold_in(own, dim), (blocks,), jnp.float32, smallest / len(split), top_value / len(split)))
        loudness = loudness * jnp.repeat(steps, shape[dim] // blocks).reshape([-1 if axis == dim else 1 for axis in range(len(shape))])
    return loudness


def gaussian(own_key, shape, spread, most, split=(), held_as=jnp.bfloat16):
    level = levels(own_key, shape, split, -0.22, 0.18) if split else 1.0
    values = jax.random.normal(own_key, shape, jnp.float32) * spread * level
    return jnp.minimum(jnp.maximum(values, -most), most).astype(held_as)


def bell_draw_with(rng, extent, deviation, bound, split, heavy, kind=jnp.bfloat16):
    values = deviation * jax.random.normal(rng, extent, jnp.float32)
    if split:
        values = values * levels(rng, extent, split, -0.22, 0.18)
    return jnp.clip(spiked(values, jax.random.fold_in(rng, 3), *heavy), -bound, bound).astype(kind)


def setup_inputs(seed: int = 0) -> dict:
    seeds = jax.random.split(jax.random.key(seed), 4)
    return {
        "lambda_amps": bell_draw_with(seeds[0], (NPAIR, NV, NV), (NPAIR * NV) ** -0.5, 0.0234375, ((0, 4), (1, 8)), (1, 2, 8, 2.0)),
        "t2_amps": gaussian(seeds[1], (NPAIR, NV, NV), 1.0, 6.0, ((0, 4), (1, 8))),
        "chol_ov": gaussian(seeds[2], (NAUX, OCC, NV), NV ** -0.5, 0.1875, ((0, 4), (2, 8))),
    }


def reference(lambda_amps, t2_amps, chol_ov):
    def add_pair(total, pieces):
        left, right = pieces
        term = lax.dot_general(left, right, (((0,), (0,)), ((), ())), preferred_element_type=jnp.float32)
        return total + term, None

    start = jnp.zeros((NV, NV), jnp.float32)
    vv, unused = lax.scan(add_pair, start, (lambda_amps, t2_amps))
    vv_low = vv.astype(jnp.bfloat16)
    flat = chol_ov.reshape(NAUX * OCC, NV)
    result = lax.dot_general(flat, vv_low, (((1,), (1,)), ((), ())), preferred_element_type=jnp.float32)
    return result.reshape(NAUX, OCC, NV).astype(jnp.bfloat16)
```

```python
import functools

import jax
import jax.numpy as jnp
from jax import lax
from jax.experimental import pallas as pl
from jax.experimental.pallas import tpu as pltpu
from jax.sharding import PartitionSpec as P

VMEM_LIMIT = 56 * 2**20


def swap(array, axis, size, offset):
    return lax.ppermute(array, axis, [(i, i ^ offset) for i in range(size)])


def depth_chunks(depth):
    step = 1280
    first = 512
    if depth <= first + step:
        return [(0, depth)]
    cuts = [0] + list(range(first, depth, step)) + [depth]
    return [(a, b - a) for a, b in zip(cuts, cuts[1:])]


def pair_kernel(chunks, rows, left_hbm, right_hbm, keep_ref, send_ref, left, right, total, sems):
    core = lax.axis_index("virt") % 2
    copies = []
    for n, (start, size) in enumerate(chunks):
        span = pl.ds(start, size)
        pair = (
            pltpu.make_async_copy(left_hbm.at[span], left.at[span], sems.at[0, n]),
            pltpu.make_async_copy(right_hbm.at[span], right.at[span], sems.at[1, n]),
        )
        for copy in pair:
            copy.start()
        copies.append(pair)
    for n, (start, size) in enumerate(chunks):
        for copy in copies[n]:
            copy.wait()
        span = pl.ds(start, size)
        term = lax.dot_general(
            left[span], right[span], (((0,), (0,)), ((), ())), preferred_element_type=jnp.float32
        )
        if n == 0:
            total[...] = term
        else:
            total[...] += term
    for mine in range(2):

        @pl.when(core == mine)
        def _():
            for chip in range(keep_ref.shape[0]):
                keep_ref[chip] = total[pl.ds((2 * chip + mine) * rows, rows)]
                send_ref[chip] = total[pl.ds((2 * chip + 1 - mine) * rows, rows)].astype(
                    send_ref.dtype
                )


def pair_product(left, right, rows):
    depth, full = left.shape
    width = right.shape[1]
    chips = full // rows // 2
    chunks = depth_chunks(depth)
    return pl.pallas_call(
        functools.partial(pair_kernel, chunks, rows),
        out_shape=(
            jax.ShapeDtypeStruct((chips, rows, width), jnp.float32),
            jax.ShapeDtypeStruct((chips, rows, width), jnp.bfloat16),
        ),
        in_specs=[pl.BlockSpec(memory_space=pl.ANY)] * 2,
        out_specs=(pl.BlockSpec(memory_space=pltpu.VMEM),) * 2,
        scratch_shapes=[
            pltpu.VMEM((depth, full), left.dtype),
            pltpu.VMEM((depth, width), right.dtype),
            pltpu.VMEM((full, width), jnp.float32),
            pltpu.SemaphoreType.DMA((2, len(chunks))),
        ],
        compiler_params=pltpu.CompilerParams(vmem_limit_bytes=VMEM_LIMIT),
        cost_estimate=pl.CostEstimate(
            flops=2 * depth * full * width,
            bytes_accessed=2 * depth * (full + width) + 6 * full * width // 2,
            transcendentals=0,
        ),
    )(left, right)


def density_kernel(count, rows, vv_ref, *refs):
    blocks, out_ref, low = refs[:count], refs[count], refs[count + 1]
    me = lax.axis_index("virt")

    @pl.when(pl.program_id(0) == 0)
    def _():
        turned = vv_ref[...].T
        for k in range(count):
            for v in range(count):

                @pl.when((me ^ k) == v)
                def _():
                    low[pl.ds(k * rows, rows)] = turned[v * rows : (v + 1) * rows].astype(low.dtype)

    flat = jnp.concatenate([block[0] for block in blocks], axis=0)
    out_ref[0] = lax.dot_general(
        low[...], flat, (((0,), (0,)), ((), ())), preferred_element_type=jnp.float32
    ).astype(out_ref.dtype)


def density_product(vv, blocks):
    rows, full = vv.shape
    occ, _, vectors = blocks[0].shape
    count = len(blocks)
    block = pl.BlockSpec((1, rows, vectors), lambda i: (i, 0, 0))
    return pl.pallas_call(
        functools.partial(density_kernel, count, rows),
        grid=(occ,),
        out_shape=jax.ShapeDtypeStruct((occ, rows, vectors), jnp.bfloat16),
        in_specs=[pl.BlockSpec((rows, full), lambda i: (0, 0))] + [block] * count,
        out_specs=block,
        scratch_shapes=[pltpu.VMEM((full, rows), jnp.bfloat16)],
        compiler_params=pltpu.CompilerParams(vmem_limit_bytes=VMEM_LIMIT),
        cost_estimate=pl.CostEstimate(
            flops=2 * occ * rows * full * vectors,
            bytes_accessed=2 * occ * vectors * (full + rows),
            transcendentals=0,
        ),
    )(vv, *blocks)


def gather_blocks(own, count):
    bits = [1 << b for b in range(1, count.bit_length() - 1)]
    pieces = jnp.split(own, len(bits), axis=0) if len(bits) > 1 else [own]
    held = [{0: piece} for piece in pieces]
    for step in range(len(bits)):
        for n, piece in enumerate(held):
            bit = bits[(n + step) % len(bits)]
            for k in list(piece):
                piece[k ^ bit] = swap(piece[k], "virt", count, bit)
    for piece in held:
        for k in list(piece):
            piece[k ^ 1] = swap(piece[k], "virt", count, 1)
    return [jnp.concatenate([piece[k] for piece in held], axis=0) for k in range(count)]


def shards(count, groups, lambda_amps, t2_amps, chol_ov):
    vectors, occ, rows = chol_ov.shape
    full = lambda_amps.shape[2]
    own = jnp.transpose(chol_ov, (1, 2, 0))
    blocks = gather_blocks(own, count)
    left = lambda_amps.reshape(-1, full)
    right = t2_amps.reshape(-1, full)
    keep, send = pair_product(left, right, rows)
    summed = keep + swap(send, "virt", count, 1)
    chip = lax.axis_index("virt") // 2
    vv = lax.dynamic_index_in_dim(summed, chip, keepdims=False)
    for k in range(1, count // 2):
        part = lax.dynamic_index_in_dim(summed, chip ^ k, keepdims=False)
        vv = vv + swap(part.astype(jnp.bfloat16), "virt", count, 2 * k)
    step = 1
    while step < groups:
        vv = vv + swap(vv.astype(jnp.bfloat16), "pair", groups, step)
        step *= 2
    if rows % 16 == 0:
        density = density_product(vv, blocks)
    else:
        me = lax.axis_index("virt")
        low = vv.astype(jnp.bfloat16).reshape(rows, count, rows)
        density = sum(
            jnp.einsum(
                "ab,ibq->iaq",
                lax.dynamic_index_in_dim(low, me ^ k, axis=1, keepdims=False),
                blocks[k],
                preferred_element_type=jnp.float32,
            )
            for k in range(count)
        ).astype(jnp.bfloat16)
    return jnp.transpose(density, (2, 0, 1))


def solution(mesh):
    placed = (P("pair", "virt", None), P("pair", "virt", None), P("pair", None, "virt"))
    step = functools.partial(shards, mesh.shape["virt"], mesh.shape["pair"])
    return jax.shard_map(
        step, mesh=mesh, in_specs=placed, out_specs=P("pair", None, "virt"), check_vma=False
    )
```

```python
import functools

import jax
import jax.numpy as jnp
from jax import lax
from jax.experimental import pallas as pl
from jax.experimental.pallas import tpu as pltpu
from jax.sharding import PartitionSpec as P

EARLY = 3
PAIR_VMEM = 40 * 2**20


def swap(array, axis, size, offset):
    return lax.ppermute(array, axis, [(i, i ^ offset) for i in range(size)])


def depth_chunks(depth):
    step = 1408
    first = 256
    if depth <= first + step:
        return [(0, depth)]
    cuts = [0] + list(range(first, depth, step)) + [depth]
    return [(a, b - a) for a, b in zip(cuts, cuts[1:])]


def pair_kernel(chunks, rows, left_hbm, right_hbm, *refs):
    *outs, left, right, total, sems = refs
    me = lax.axis_index("virt")
    count = len(outs)
    copies = []
    for n, (start, size) in enumerate(chunks):
        span = pl.ds(start, size)
        pair = (
            pltpu.make_async_copy(left_hbm.at[span], left.at[span], sems.at[0, n]),
            pltpu.make_async_copy(right_hbm.at[span], right.at[span], sems.at[1, n]),
        )
        for copy in pair:
            copy.start()
        copies.append(pair)
    for n, (start, size) in enumerate(chunks):
        for copy in copies[n]:
            copy.wait()
        span = pl.ds(start, size)
        term = lax.dot_general(
            left[span], right[span], (((0,), (0,)), ((), ())), preferred_element_type=jnp.float32
        )
        if n == 0:
            total[...] = term
        else:
            total[...] += term
    for mine in range(count):

        @pl.when(me == mine)
        def _():
            for k, out in enumerate(outs):
                block = total[pl.ds((mine ^ k) * rows, rows)]
                out[...] = block.astype(out.dtype)


def pair_product(left, right, rows):
    depth, full = left.shape
    width = right.shape[1]
    count = full // rows
    chunks = depth_chunks(depth)
    kinds = [jnp.bfloat16 if k % 2 else jnp.float32 for k in range(count)]
    return pl.pallas_call(
        functools.partial(pair_kernel, chunks, rows),
        out_shape=[pltpu.VMEM((rows, width), kind) for kind in kinds],
        in_specs=[pl.BlockSpec(memory_space=pltpu.HBM)] * 2,
        out_specs=[pl.BlockSpec(memory_space=pltpu.VMEM)] * count,
        scratch_shapes=[
            pltpu.VMEM((depth, full), left.dtype),
            pltpu.VMEM((depth, width), right.dtype),
            pltpu.VMEM((full, width), jnp.float32),
            pltpu.SemaphoreType.DMA((2, len(chunks))),
        ],
        compiler_params=pltpu.CompilerParams(vmem_limit_bytes=PAIR_VMEM),
        cost_estimate=pl.CostEstimate(
            flops=2 * depth * full * width,
            bytes_accessed=2 * depth * (full + width) + 3 * full * width,
            transcendentals=0,
        ),
    )(*[pltpu.with_memory_space_constraint(side, pltpu.HBM) for side in (left, right)])


def fold_kernel(count, *refs):
    half = count // 2
    terms, arrived, outs = refs[:half], refs[half:count], refs[len(refs) - half :]
    for term, other, out in zip(terms, arrived, outs):
        out[...] = (term[...] + other[...].astype(jnp.float32)).astype(out.dtype)


def fold(terms, arrived, after):
    count = 2 * len(terms)
    shape = terms[0].shape
    kinds = [jnp.float32] + [jnp.bfloat16] * (len(terms) - 1)
    return pl.pallas_call(
        functools.partial(fold_kernel, count),
        out_shape=[pltpu.VMEM(shape, kind) for kind in kinds],
        in_specs=[pl.BlockSpec(memory_space=pltpu.VMEM)] * count
        + [pl.BlockSpec(memory_space=pl.ANY)] * len(after),
        out_specs=[pl.BlockSpec(memory_space=pltpu.VMEM)] * len(terms),
        compiler_params=pltpu.CompilerParams(vmem_limit_bytes=8 * 2**20),
        cost_estimate=pl.CostEstimate(flops=0, bytes_accessed=0, transcendentals=0),
    )(*terms, *arrived, *after)


def pass_kernel(*refs):
    pass


def hold(arrays, after):
    return pl.pallas_call(
        pass_kernel,
        out_shape=[jax.ShapeDtypeStruct(array.shape, array.dtype) for array in arrays],
        in_specs=[pl.BlockSpec(memory_space=pl.ANY)] * (len(arrays) + len(after)),
        out_specs=[pl.BlockSpec(memory_space=pl.ANY)] * len(arrays),
        input_output_aliases={n: n for n in range(len(arrays))},
        compiler_params=pltpu.CompilerParams(vmem_limit_bytes=2**20),
        cost_estimate=pl.CostEstimate(flops=0, bytes_accessed=0, transcendentals=0),
    )(*arrays, *after)


def density_kernel(count, rows, splits, vv_ref, *refs):
    total = sum(len(s) for s in splits)
    parts, out_ref, low = refs[:total], refs[total], refs[total + 1]
    me = lax.axis_index("virt")
    step = pl.program_id(0)

    @pl.when(step == 0)
    def _():
        turned = vv_ref[...].T
        for k in range(count):
            for v in range(count):

                @pl.when((me ^ k) == v)
                def _():
                    low[pl.ds(k * rows, rows)] = turned[v * rows : (v + 1) * rows].astype(low.dtype)

    flat, at = [], 0
    for split in splits:
        block = parts[at][0]
        for n in range(1, len(split)):
            block = jnp.where(step < split[n], block, parts[at + n][0])
        flat.append(block)
        at += len(split)
    out_ref[0] = lax.dot_general(
        low[...],
        jnp.concatenate(flat, axis=0),
        (((0,), (0,)), ((), ())),
        preferred_element_type=jnp.float32,
    ).astype(out_ref.dtype)


def density_product(vv, blocks):
    rows, full = vv.shape
    count = len(blocks)
    vectors = blocks[0][0].shape[2]
    occ = sum(part.shape[0] for part in blocks[0])
    splits, specs = [], []
    for block in blocks:
        start, split = 0, []
        for part in block:
            size = part.shape[0]
            split.append(start)
            specs.append(
                pl.BlockSpec(
                    (1, rows, vectors),
                    lambda i, start=start, size=size: (jnp.clip(i - start, 0, size - 1), 0, 0),
                )
            )
            start += size
        splits.append(split)
    return pl.pallas_call(
        functools.partial(density_kernel, count, rows, splits),
        grid=(occ,),
        out_shape=jax.ShapeDtypeStruct((occ, rows, vectors), jnp.bfloat16),
        in_specs=[pl.BlockSpec((rows, full), lambda i: (0, 0))] + specs,
        out_specs=pl.BlockSpec((1, rows, vectors), lambda i: (i, 0, 0)),
        scratch_shapes=[pltpu.VMEM((full, rows), jnp.bfloat16)],
        compiler_params=pltpu.CompilerParams(vmem_limit_bytes=24 * 2**20),
        cost_estimate=pl.CostEstimate(flops=0, bytes_accessed=0, transcendentals=0),
    )(vv, *[part for block in blocks for part in block])


def send_early(own, count, early):
    occ = own.shape[0]
    early = min(early, occ)
    bits = [k for k in range(2, count) if k & (k - 1) == 0]
    start = {k: occ - early if k == 2 else 0 for k in bits}
    came = {k: swap(own[start[k] : start[k] + early], "virt", count, k) for k in bits}
    rest = {k: own[: occ - early] if k == 2 else own[early:] for k in bits}
    return came, {k: part for k, part in rest.items() if part.shape[0]}


def gather_rest(own, came, rest, count):
    occ = own.shape[0]
    half = (occ + 1) // 2
    held = {0: [own]}
    for k in sorted(range(2, count, 2), key=lambda k: (bin(k).count("1"), k)):
        low_bit, high_bit = k & -k, 1 << (k.bit_length() - 1)
        if k in came:
            parts = [came[k]] + ([swap(rest[k], "virt", count, k)] if k in rest else [])
            held[k] = parts[::-1] if k == 2 else parts
        else:
            held[k] = [swap(take(held[k ^ high_bit], half, occ), "virt", count, high_bit)]
            if half < occ:
                held[k].insert(0, swap(take(held[k ^ low_bit], 0, half), "virt", count, low_bit))
    return held


def take(parts, start, stop):
    kept, at = [], 0
    for part in parts:
        size = part.shape[0]
        low, high = max(start - at, 0), min(stop - at, size)
        if low < high:
            kept.append(part[low:high])
        at += size
    return kept[0] if len(kept) == 1 else jnp.concatenate(kept, axis=0)


def shards(count, groups, lambda_amps, t2_amps, chol_ov):
    rows = chol_ov.shape[2]
    full = lambda_amps.shape[2]
    own = jnp.transpose(chol_ov, (1, 2, 0))
    came, rest = send_early(own, count, EARLY)
    left = lambda_amps.reshape(-1, full)
    right = t2_amps.reshape(-1, full)
    terms = pair_product(left, right, rows)
    even = range(0, count, 2)
    arrived = [swap(terms[k ^ 1], "virt", count, 1) for k in even]
    sums = fold([terms[k] for k in even], arrived, list(came.values()))
    arrived = [swap(sums[k // 2], "virt", count, k) for k in range(2, count, 2)]
    kept = hold([*came.values(), *rest.values()], arrived)
    came = dict(zip(came, kept))
    rest = dict(zip(rest, kept[len(came) :]))
    held = gather_rest(own, came, rest, count)
    vv = sums[0]
    for part in arrived:
        vv = vv + part
    step = 1
    while step < groups:
        part = swap(vv.astype(jnp.bfloat16), "pair", groups, step)
        vv = vv + part
        step *= 2
    names = [(k, n) for k in held for n in range(len(held[k]))]
    late = [(k, n) for k, n in names if k and not (k in came and held[k][n] is came[k])]
    kept = hold([held[k][n] for k, n in late], [part])
    for (k, n), array in zip(late, kept):
        held[k][n] = array
    for k in list(held):
        held[k ^ 1] = [swap(array, "virt", count, 1) for array in held[k]]
    blocks = [held[k] for k in range(count)]
    if rows % 16 == 0:
        density = density_product(vv, blocks)
    else:
        me = lax.axis_index("virt")
        low = vv.astype(jnp.bfloat16).reshape(rows, count, rows)
        density = sum(
            jnp.einsum(
                "ab,ibq->iaq",
                lax.dynamic_index_in_dim(low, me ^ k, axis=1, keepdims=False),
                jnp.concatenate(blocks[k], axis=0),
                preferred_element_type=jnp.float32,
            )
            for k in range(count)
        ).astype(jnp.bfloat16)
    return jnp.transpose(density, (2, 0, 1))


def solution(mesh):
    placed = (P("pair", "virt", None), P("pair", "virt", None), P("pair", None, "virt"))
    step = functools.partial(shards, mesh.shape["virt"], mesh.shape["pair"])
    return jax.shard_map(
        step, mesh=mesh, in_specs=placed, out_specs=P("pair", None, "virt"), check_vma=False
    )
```

```python
import functools

import jax
import jax.numpy as jnp
from jax import lax
from jax.experimental import pallas as pl
from jax.experimental.pallas import tpu as pltpu
from jax.sharding import PartitionSpec as P

AHEAD = 3
PAIR_VMEM = 40 * 2**20
SMALL_VMEM = 12 * 2**20
HBM = pl.BlockSpec(memory_space=pltpu.HBM)
VMEM = pl.BlockSpec(memory_space=pltpu.VMEM)
ANY = pl.BlockSpec(memory_space=pl.ANY)
FREE = pl.CostEstimate(flops=0, bytes_accessed=0, transcendentals=0)
LONG = pl.CostEstimate(flops=10**10, bytes_accessed=0, transcendentals=0)


def swap(array, axis, size, offset):
    return lax.ppermute(array, axis, [(i, i ^ offset) for i in range(size)])


def in_vmem(arrays):
    return [pltpu.with_memory_space_constraint(array, pltpu.VMEM) for array in arrays]


def depth_chunks(depth):
    cuts = [0]
    for size in (256, 512, 1024, 1280):
        if cuts[-1] + size < depth:
            cuts.append(cuts[-1] + size)
    while depth - cuts[-1] > 2048:
        cuts.append(cuts[-1] + 1024)
    return [(a, b - a) for a, b in zip(cuts, cuts[1:] + [depth])]


def pair_kernel(chunks, left_hbm, right_hbm, own_hbm, total, own_ref, left, right, sems, own_sem):
    copies = []
    for n, (start, size) in enumerate(chunks):
        span = pl.ds(start, size)
        pair = (
            pltpu.make_async_copy(left_hbm.at[span], left.at[span], sems.at[0, n]),
            pltpu.make_async_copy(right_hbm.at[span], right.at[span], sems.at[1, n]),
        )
        copies.append(pair)
    own_copy = pltpu.make_async_copy(own_hbm, own_ref, own_sem)
    copies.append((own_copy,))
    for copy in [copy for pair in copies[:AHEAD] for copy in pair]:
        copy.start()
    for n, (start, size) in enumerate(chunks):
        for copy in copies[n]:
            copy.wait()
        for copy in [copy for pair in copies[n + AHEAD : n + AHEAD + 1] for copy in pair]:
            copy.start()
        span = pl.ds(start, size)
        term = lax.dot_general(
            left[span], right[span], (((0,), (0,)), ((), ())), preferred_element_type=jnp.float32
        )
        if n == 0:
            total[...] = term
        else:
            total[...] += term
    own_copy.wait()


def pair_product(left, right, own):
    depth, full = left.shape
    chunks = depth_chunks(depth)
    return pl.pallas_call(
        functools.partial(pair_kernel, chunks),
        out_shape=[pltpu.VMEM((full, full), jnp.float32), pltpu.VMEM(own.shape, own.dtype)],
        in_specs=[HBM] * 3,
        out_specs=[VMEM] * 2,
        scratch_shapes=[
            pltpu.VMEM((depth, full), left.dtype),
            pltpu.VMEM((depth, full), right.dtype),
            pltpu.SemaphoreType.DMA((2, len(chunks))),
            pltpu.SemaphoreType.DMA,
        ],
        compiler_params=pltpu.CompilerParams(vmem_limit_bytes=PAIR_VMEM),
        cost_estimate=pl.CostEstimate(
            flops=2 * depth * full * full, bytes_accessed=4 * depth * full, transcendentals=0
        ),
    )(*[pltpu.with_memory_space_constraint(side, pltpu.HBM) for side in (left, right, own)])


def cut_kernel(rows, parity, total, *outs):
    me = lax.axis_index("virt")
    chips = len(outs)
    for mine in range(2 * chips):

        @pl.when(me == mine)
        def _():
            for k, out in enumerate(outs):
                chip, core = (mine >> 1) ^ k, (mine & 1) ^ parity
                pieces = []
                for side in range(2):
                    a = 2 * chip + (side ^ core)
                    for offset in range(chips):
                        b = 2 * (chip ^ offset) + core
                        pieces.append(total[a * rows : (a + 1) * rows, b * rows : (b + 1) * rows])
                out[...] = jnp.concatenate(pieces, axis=1).astype(out.dtype)


def cut(total, rows, parity, kind):
    full = total.shape[0]
    chips = full // rows // 2
    return pl.pallas_call(
        functools.partial(cut_kernel, rows, parity),
        out_shape=[pltpu.VMEM((rows, full), kind)] * chips,
        in_specs=[VMEM],
        out_specs=[VMEM] * chips,
        compiler_params=pltpu.CompilerParams(vmem_limit_bytes=SMALL_VMEM),
        cost_estimate=FREE,
    )(*in_vmem([total]))


def fold_kernel(half, *refs):
    terms, arrived, outs = refs[:half], refs[half : 2 * half], refs[len(refs) - half :]
    for term, other, out in zip(terms, arrived, outs):
        out[...] = (term[...] + other[...].astype(jnp.float32)).astype(out.dtype)


def fold(terms, arrived, after):
    shape = terms[0].shape
    kinds = [jnp.float32] + [jnp.bfloat16] * (len(terms) - 1)
    return pl.pallas_call(
        functools.partial(fold_kernel, len(terms)),
        out_shape=[pltpu.VMEM(shape, kind) for kind in kinds],
        in_specs=[VMEM] * (2 * len(terms)) + [ANY] * len(after),
        out_specs=[VMEM] * len(terms),
        compiler_params=pltpu.CompilerParams(vmem_limit_bytes=SMALL_VMEM),
        cost_estimate=FREE,
    )(*in_vmem([*terms, *arrived]), *after)


def total_kernel(parts, *refs):
    wide, narrow = refs[-2:]
    total = refs[0][...]
    for ref in refs[1:parts]:
        total += ref[...].astype(jnp.float32)
    wide[...] = total
    narrow[...] = total.astype(narrow.dtype)


def total(parts, after, flops=0):
    shape = parts[0].shape
    return pl.pallas_call(
        functools.partial(total_kernel, len(parts)),
        out_shape=[pltpu.VMEM(shape, jnp.float32), pltpu.VMEM(shape, jnp.bfloat16)],
        in_specs=[VMEM] * len(parts) + [ANY] * len(after),
        out_specs=[VMEM] * 2,
        compiler_params=pltpu.CompilerParams(vmem_limit_bytes=SMALL_VMEM),
        cost_estimate=pl.CostEstimate(flops=flops, bytes_accessed=0, transcendentals=0),
    )(*in_vmem(parts), *after)


def low_kernel(vv_ref, part_ref, low_ref):
    rows, full = vv_ref.shape
    whole = vv_ref[...] + part_ref[...].astype(jnp.float32)
    for side in range(2):
        half = whole[:, side * (full // 2) : (side + 1) * (full // 2)]
        low_ref[side * rows : (side + 1) * rows] = half.astype(low_ref.dtype)


def low_rows(vv, part):
    rows, full = vv.shape
    return pl.pallas_call(
        low_kernel,
        out_shape=pltpu.VMEM((2 * rows, full // 2), jnp.bfloat16),
        in_specs=[VMEM] * 2,
        out_specs=VMEM,
        compiler_params=pltpu.CompilerParams(vmem_limit_bytes=SMALL_VMEM),
        cost_estimate=FREE,
    )(*in_vmem([vv, part]))


def pass_kernel(*refs):
    pass


def hold(arrays, after, cost):
    return pl.pallas_call(
        pass_kernel,
        out_shape=[jax.ShapeDtypeStruct(array.shape, array.dtype) for array in arrays],
        in_specs=[ANY] * (len(arrays) + len(after)),
        out_specs=[ANY] * len(arrays),
        input_output_aliases={n: n for n in range(len(arrays))},
        compiler_params=pltpu.CompilerParams(vmem_limit_bytes=2**20),
        cost_estimate=cost,
    )(*arrays, *after)


def density_kernel(spans, low_ref, *refs):
    *blocks, mine_ref, theirs_ref = refs
    rows = mine_ref.shape[1]
    for i in range(mine_ref.shape[0]):
        flat = jnp.concatenate([block[start + i] for block, start in zip(blocks, spans)], axis=0)
        both = jnp.dot(low_ref[...], flat, preferred_element_type=jnp.float32)
        mine_ref[i] = both[:rows]
        theirs_ref[i] = both[rows:].astype(theirs_ref.dtype)


def density_product(low, blocks, count):
    rows = low.shape[0] // 2
    vectors = blocks[0][0].shape[2]
    shape = (count, rows, vectors)
    return pl.pallas_call(
        functools.partial(density_kernel, [start for _, start in blocks]),
        out_shape=[pltpu.VMEM(shape, jnp.float32), pltpu.VMEM(shape, jnp.bfloat16)],
        in_specs=[VMEM] * (1 + len(blocks)),
        out_specs=[VMEM] * 2,
        compiler_params=pltpu.CompilerParams(vmem_limit_bytes=SMALL_VMEM),
        cost_estimate=FREE,
    )(*in_vmem([low, *[array for array, _ in blocks]]))


def join_kernel(mine_ref, arrived_ref, *refs):
    i = pl.program_id(0)
    refs[-1][0] = (mine_ref[i] + arrived_ref[i].astype(jnp.float32)).astype(refs[-1].dtype)


def join(mine, arrived, occ, start, base):
    count, rows, vectors = mine.shape
    given = [] if base is None else [base]
    return pl.pallas_call(
        join_kernel,
        grid=(count,),
        out_shape=jax.ShapeDtypeStruct((occ, rows, vectors), jnp.bfloat16),
        in_specs=[VMEM] * 2 + [ANY] * len(given),
        out_specs=pl.BlockSpec((1, rows, vectors), lambda i: (i + start, 0, 0)),
        input_output_aliases={2: 0} if given else {},
        compiler_params=pltpu.CompilerParams(vmem_limit_bytes=SMALL_VMEM),
        cost_estimate=FREE,
    )(*in_vmem([mine, arrived]), *given)


def permuted(count, groups, lambda_amps, t2_amps, chol_ov):
    rows, full = chol_ov.shape[2], lambda_amps.shape[2]
    own = jnp.transpose(chol_ov, (1, 2, 0))
    occ = own.shape[0]
    half = occ // 2
    bits = [k for k in range(2, count) if k & (k - 1) == 0]
    came = {k: swap(own, "virt", count, k) for k in bits}

    product, own = pair_product(lambda_amps.reshape(-1, full), t2_amps.reshape(-1, full), own)
    even = range(0, count, 2)
    arrived = [swap(part, "virt", count, 1) for part in cut(product, rows, 1, jnp.bfloat16)]
    sums = fold(cut(product, rows, 0, jnp.float32), arrived, [])
    arrived = [swap(sums[k // 2], "virt", count, k) for k in range(2, count, 2)]
    vv, narrow = total([sums[0], *arrived], list(came.values()))
    came = dict(zip(bits, hold(list(came.values()), arrived[:1], FREE)))

    held = {0: [(own, 0), (own, half)]} | {k: [(came[k], 0), (came[k], half)] for k in bits}
    for k in sorted(set(even) - set(held), key=lambda k: (bin(k).count("1"), k)):
        low_bit, high_bit = k & -k, 1 << (k.bit_length() - 1)
        lower, start = held[k ^ low_bit][0]
        upper, middle = held[k ^ high_bit][1]
        lower = lower[start : start + half]
        upper = upper[middle : middle + occ - half]
        held[k] = [
            (swap(lower, "virt", count, low_bit), 0),
            (swap(upper, "virt", count, high_bit), 0),
        ]
    step = 1
    while step < groups:
        part = swap(narrow, "pair", groups, step)
        if 2 * step < groups:
            vv, narrow = total([vv, part], [], 2 * 10**9)
        step *= 2
    low = low_rows(vv, part)
    parts = []
    for n, size in enumerate((half, occ - half)):
        mine, theirs = density_product(low, [held[k][n] for k in even], size)
        parts.append((mine, swap(theirs, "virt", count, 1), occ, n * half))
    density = None
    for part in parts:
        density = join(*part, density)
    return jnp.transpose(density, (2, 0, 1))


def gathered(lambda_amps, t2_amps, chol_ov):
    vv = lax.dot_general(
        lambda_amps, t2_amps, (((0, 1), (0, 1)), ((), ())), preferred_element_type=jnp.float32
    )
    vv = lax.psum_scatter(vv, "virt", scatter_dimension=0, tiled=True)
    low = lax.psum(vv, "pair").astype(jnp.bfloat16)
    blocks = lax.all_gather(jnp.transpose(chol_ov, (1, 2, 0)), "virt", axis=1, tiled=True)
    density = jnp.einsum("ab,ibq->iaq", low, blocks, preferred_element_type=jnp.float32)
    return jnp.transpose(density, (2, 0, 1)).astype(jnp.bfloat16)


def solution(mesh):
    count, groups = mesh.shape["virt"], mesh.shape["pair"]
    paired = count & (count - 1) == 0 and groups & (groups - 1) == 0 and count > 3 and groups > 1

    def shards(lambda_amps, t2_amps, chol_ov):
        if paired and chol_ov.shape[2] % 16 == 0 and chol_ov.shape[1] > 1:
            return permuted(count, groups, lambda_amps, t2_amps, chol_ov)
        return gathered(lambda_amps, t2_amps, chol_ov)

    placed = (P("pair", "virt", None), P("pair", "virt", None), P("pair", None, "virt"))
    return jax.shard_map(
        shards, mesh=mesh, in_specs=placed, out_specs=P("pair", None, "virt"), check_vma=False
    )
```

```python
import functools

import jax
import jax.numpy as jnp
from jax import lax
from jax.experimental import pallas as pl
from jax.experimental.pallas import tpu as pltpu
from jax.sharding import PartitionSpec as P

AHEAD = 3
PAIR_VMEM = 40 * 2**20
SMALL_VMEM = 12 * 2**20
HBM = pl.BlockSpec(memory_space=pltpu.HBM)
VMEM = pl.BlockSpec(memory_space=pltpu.VMEM)
ANY = pl.BlockSpec(memory_space=pl.ANY)
FREE = pl.CostEstimate(flops=0, bytes_accessed=0, transcendentals=0)


def filler(gigaflops):
    return pl.CostEstimate(flops=int(gigaflops * 10**9), bytes_accessed=0, transcendentals=0)


PLANE_FILL = (filler(5), filler(1))
GROUP_FILL = (filler(2), filler(2))
LAST_FILL = filler(10)


def swap(array, axis, size, offset):
    return lax.ppermute(array, axis, [(i, i ^ offset) for i in range(size)])


def in_vmem(arrays):
    return [pltpu.with_memory_space_constraint(array, pltpu.VMEM) for array in arrays]


def depth_chunks(depth):
    cuts = [0]
    for size in (256, 512, 1024, 1280):
        if cuts[-1] + size < depth:
            cuts.append(cuts[-1] + size)
    while depth - cuts[-1] > 2048:
        cuts.append(cuts[-1] + 1024)
    return [(a, b - a) for a, b in zip(cuts, cuts[1:] + [depth])]


def pair_kernel(chunks, left_hbm, right_hbm, own_hbm, total, own_ref, left, right, sems, own_sem):
    copies = []
    for n, (start, size) in enumerate(chunks):
        span = pl.ds(start, size)
        pair = (
            pltpu.make_async_copy(left_hbm.at[span], left.at[span], sems.at[0, n]),
            pltpu.make_async_copy(right_hbm.at[span], right.at[span], sems.at[1, n]),
        )
        copies.append(pair)
    own_copy = pltpu.make_async_copy(own_hbm, own_ref, own_sem)
    copies.append((own_copy,))
    for copy in [copy for pair in copies[:AHEAD] for copy in pair]:
        copy.start()
    for n, (start, size) in enumerate(chunks):
        for copy in copies[n]:
            copy.wait()
        for copy in [copy for pair in copies[n + AHEAD : n + AHEAD + 1] for copy in pair]:
            copy.start()
        span = pl.ds(start, size)
        term = lax.dot_general(
            left[span], right[span], (((0,), (0,)), ((), ())), preferred_element_type=jnp.float32
        )
        if n == 0:
            total[...] = term
        else:
            total[...] += term
    own_copy.wait()


def pair_product(left, right, own):
    depth, full = left.shape
    chunks = depth_chunks(depth)
    return pl.pallas_call(
        functools.partial(pair_kernel, chunks),
        out_shape=[pltpu.VMEM((full, full), jnp.float32), pltpu.VMEM(own.shape, own.dtype)],
        in_specs=[HBM] * 3,
        out_specs=[VMEM] * 2,
        scratch_shapes=[
            pltpu.VMEM((depth, full), left.dtype),
            pltpu.VMEM((depth, full), right.dtype),
            pltpu.SemaphoreType.DMA((2, len(chunks))),
            pltpu.SemaphoreType.DMA,
        ],
        compiler_params=pltpu.CompilerParams(vmem_limit_bytes=PAIR_VMEM),
        cost_estimate=pl.CostEstimate(
            flops=2 * depth * full * full, bytes_accessed=4 * depth * full, transcendentals=0
        ),
    )(*[pltpu.with_memory_space_constraint(side, pltpu.HBM) for side in (left, right, own)])


def cut_kernel(rows, parity, total, *outs):
    me = lax.axis_index("virt")
    chips = outs[0].shape[0]
    for mine in range(2 * chips):

        @pl.when(me == mine)
        def _():
            core = (mine & 1) ^ parity
            for side, out in enumerate(outs):
                for k in range(chips):
                    chip = (mine >> 1) ^ k
                    first = (2 * chip + (side ^ core)) * rows
                    pieces = []
                    for a in (first, first + rows // 2):
                        for offset in range(chips):
                            b = (2 * (chip ^ offset) + core) * rows
                            pieces.append(total[a : a + rows // 2, b : b + rows])
                    out[k] = jnp.concatenate(pieces, axis=1).astype(out.dtype)


def cut(total, rows, parity, kind):
    full = total.shape[0]
    chips = full // rows // 2
    return pl.pallas_call(
        functools.partial(cut_kernel, rows, parity),
        out_shape=[pltpu.VMEM((chips, rows // 2, full), kind)] * 2,
        in_specs=[VMEM],
        out_specs=[VMEM] * 2,
        compiler_params=pltpu.CompilerParams(vmem_limit_bytes=SMALL_VMEM),
        cost_estimate=FREE,
    )(*in_vmem([total]))


def merge_kernel(sent, rest, count, term, other, *refs):
    narrow, wide = refs[count:]
    for places, out in ((sent, narrow), (rest, wide)):
        for n, k in enumerate(places):
            out[n] = (term[k] + other[k].astype(jnp.float32)).astype(out.dtype)


def merge(term, other, sent, rest, after, cost):
    shape = term.shape[1:]
    return pl.pallas_call(
        functools.partial(merge_kernel, sent, rest, len(after)),
        out_shape=[
            pltpu.VMEM((len(sent), *shape), jnp.bfloat16),
            pltpu.VMEM((len(rest), *shape), jnp.float32),
        ],
        in_specs=[VMEM] * 2 + [ANY] * len(after),
        out_specs=[VMEM] * 2,
        compiler_params=pltpu.CompilerParams(vmem_limit_bytes=SMALL_VMEM),
        cost_estimate=cost,
    )(*in_vmem([term, other]), *after)


def low_kernel(count, vv_ref, part_ref, *refs):
    low_ref = refs[count]
    whole = vv_ref[0] + part_ref[0].astype(jnp.float32)
    half = whole.shape[1] // 2
    low_ref[...] = jnp.concatenate([whole[:, :half], whole[:, half:]], axis=0).astype(low_ref.dtype)


def low_rows(vv, part, after, cost):
    _, rows, full = vv.shape
    return pl.pallas_call(
        functools.partial(low_kernel, len(after)),
        out_shape=pltpu.VMEM((2 * rows, full // 2), jnp.bfloat16),
        in_specs=[VMEM] * 2 + [ANY] * len(after),
        out_specs=VMEM,
        compiler_params=pltpu.CompilerParams(vmem_limit_bytes=SMALL_VMEM),
        cost_estimate=cost,
    )(*in_vmem([vv, part]), *after)


def block_rows(blocks, place):
    return jnp.concatenate([blocks[n][at] for n, at in place], axis=0)


def places_of(blocks):
    arrays = {id(array): array for block in blocks for array, _ in block}
    index = {name: n for n, name in enumerate(arrays)}
    return list(arrays.values()), [[(index[id(array)], at) for array, at in block] for block in blocks]


def other_kernel(places, low_ref, *refs):
    *blocks, out_ref = refs
    for i, place in enumerate(places):
        out_ref[i] = jnp.dot(
            low_ref[...], block_rows(blocks, place), preferred_element_type=jnp.float32
        ).astype(out_ref.dtype)


def other_density(low, blocks):
    arrays, places = places_of(blocks)
    return pl.pallas_call(
        functools.partial(other_kernel, places),
        out_shape=pltpu.VMEM((len(blocks), low.shape[0], arrays[0].shape[2]), jnp.bfloat16),
        in_specs=[VMEM] * (1 + len(arrays)),
        out_specs=VMEM,
        compiler_params=pltpu.CompilerParams(vmem_limit_bytes=SMALL_VMEM),
        cost_estimate=FREE,
    )(*in_vmem([low, *arrays]))


def own_kernel(places, cuts, low_ref, *refs):
    *blocks, out_ref = refs
    blocks, arrived = blocks[: -len(cuts)], blocks[-len(cuts) :]
    for i, place in enumerate(places):
        n = max(n for n, start in enumerate(cuts) if start <= i)

        @pl.when(pl.program_id(0) == i)
        def _():
            both = jnp.dot(
                low_ref[...], block_rows(blocks, place), preferred_element_type=jnp.float32
            )
            both += arrived[n][i - cuts[n]].astype(jnp.float32)
            out_ref[0] = both.astype(out_ref.dtype)


def own_density(low, blocks, arrived):
    arrays, places = places_of(blocks)
    cuts = [sum(part.shape[0] for part in arrived[:n]) for n in range(len(arrived))]
    rows, vectors = low.shape[0], arrays[0].shape[2]
    return pl.pallas_call(
        functools.partial(own_kernel, places, cuts),
        grid=(len(blocks),),
        out_shape=jax.ShapeDtypeStruct((len(blocks), rows, vectors), jnp.bfloat16),
        in_specs=[VMEM] * (1 + len(arrays) + len(arrived)),
        out_specs=pl.BlockSpec((1, rows, vectors), lambda i: (i, 0, 0)),
        compiler_params=pltpu.CompilerParams(vmem_limit_bytes=SMALL_VMEM),
        cost_estimate=FREE,
    )(*in_vmem([low, *arrays, *arrived]))


def load_kernel(cuts, own_hbm, *refs):
    outs, sems = refs[:-1], refs[-1]
    copies = [
        pltpu.make_async_copy(own_hbm.at[pl.ds(start, size)], out, sems.at[n])
        for n, ((start, size), out) in enumerate(zip(cuts, outs))
    ]
    for copy in copies:
        copy.start()
    for copy in copies:
        copy.wait()


def load(own, cuts):
    return pl.pallas_call(
        functools.partial(load_kernel, cuts),
        out_shape=[pltpu.VMEM((size, *own.shape[1:]), own.dtype) for _, size in cuts],
        in_specs=[HBM],
        out_specs=[VMEM] * len(cuts),
        scratch_shapes=[pltpu.SemaphoreType.DMA((len(cuts),))],
        compiler_params=pltpu.CompilerParams(vmem_limit_bytes=SMALL_VMEM),
        cost_estimate=FREE,
    )(pltpu.with_memory_space_constraint(own, pltpu.HBM))


def lay(*arrays):
    return [(array, at) for array in arrays for at in range(array.shape[0])]


def pick(places):
    runs = []
    for array, at in places:
        if runs and runs[-1][0] is array and runs[-1][2] == at:
            runs[-1][2] = at + 1
        else:
            runs.append([array, at, at + 1])
    pieces = [array[start:stop] for array, start, stop in runs]
    return pieces[0] if len(pieces) == 1 else jnp.concatenate(pieces, axis=0)


def permuted(count, groups, lambda_amps, t2_amps, chol_ov):
    rows, full = chol_ov.shape[2], lambda_amps.shape[2]
    own = jnp.transpose(chol_ov, (1, 2, 0))
    occ = own.shape[0]
    half = occ // 2
    bits = [k for k in range(2, count) if k & (k - 1) == 0]
    even = range(0, count, 2)
    early = occ - occ // 4
    first = {k: (0, occ) if k == 2 else (0, early) for k in bits}
    pieces = sorted({cut for cut in first.values() if cut[1] < occ})
    loaded = dict(zip(pieces, load(own, pieces))) if pieces else {}
    came = {k: swap(loaded.get(first[k], own), "virt", count, k) for k in bits}

    product, own = pair_product(lambda_amps.reshape(-1, full), t2_amps.reshape(-1, full), own)
    other = [swap(part, "virt", count, 1) for part in cut(product, rows, 1, jnp.bfloat16)]
    vv = list(cut(product, rows, 0, jnp.float32))
    narrow = [None, None]
    for step in range(len(bits) + 1):
        for side in (1, 0):
            held = range(vv[side].shape[0])
            if step < len(bits):
                bit = (bits[::-1] if side else bits)[step]
                place = len(held) // 2 if side else 1
                sent = [k for k in held if k & place]
                rest = [k for k in held if not k & place]
            else:
                sent = rest = [0]
            after = list(came.values()) if (step, side) == (1, 1) else []
            cost = PLANE_FILL[side] if step == len(bits) else FREE
            narrow[side], vv[side] = merge(vv[side], other[side], sent, rest, after, cost)
            if step < len(bits):
                other[side] = swap(narrow[side], "virt", count, bit)

    held = {0: lay(own)}
    for k in bits:
        start, size = first[k]
        parts = [came[k]]
        if start:
            parts.insert(0, swap(own[:start], "virt", count, k))
        if start + size < occ:
            parts.append(swap(own[start + size :], "virt", count, k))
        held[k] = lay(*parts)
    for k in sorted(set(even) - set(held), key=lambda k: (bin(k).count("1"), k)):
        low_bit, high_bit = k & -k, 1 << (k.bit_length() - 1)
        lower = pick(held[k ^ low_bit][:half])
        upper = pick(held[k ^ high_bit][half:])
        held[k] = lay(swap(lower, "virt", count, low_bit), swap(upper, "virt", count, high_bit))
    blocks = [[held[k][i] for k in even] for i in range(occ)]

    step = 1
    while step < groups:
        part = {side: swap(narrow[side], "pair", groups, step) for side in (1, 0)}
        after = [narrow[0]]
        if 2 * step < groups:
            narrow[1], vv[1] = merge(vv[1], part[1], [0], [0], after, GROUP_FILL[1])
            narrow[0], vv[0] = merge(vv[0], part[0], [0], [0], [], GROUP_FILL[0])
        step *= 2
    low = {1: low_rows(vv[1], part[1], after, FREE), 0: low_rows(vv[0], part[0], [], LAST_FILL)}
    arrived = [
        swap(other_density(low[1], part), "virt", count, 1) for part in (blocks[:half], blocks[half:])
    ]
    return jnp.transpose(own_density(low[0], blocks, arrived), (2, 0, 1))


def gathered(lambda_amps, t2_amps, chol_ov):
    vv = lax.dot_general(
        lambda_amps, t2_amps, (((0, 1), (0, 1)), ((), ())), preferred_element_type=jnp.float32
    )
    vv = lax.psum_scatter(vv, "virt", scatter_dimension=0, tiled=True)
    low = lax.psum(vv, "pair").astype(jnp.bfloat16)
    blocks = lax.all_gather(jnp.transpose(chol_ov, (1, 2, 0)), "virt", axis=1, tiled=True)
    density = jnp.einsum("ab,ibq->iaq", low, blocks, preferred_element_type=jnp.float32)
    return jnp.transpose(density, (2, 0, 1)).astype(jnp.bfloat16)


def solution(mesh):
    count, groups = mesh.shape["virt"], mesh.shape["pair"]
    paired = count & (count - 1) == 0 and groups & (groups - 1) == 0 and count > 3 and groups > 1

    def shards(lambda_amps, t2_amps, chol_ov):
        if paired and chol_ov.shape[2] % 16 == 0 and chol_ov.shape[1] > 1:
            return permuted(count, groups, lambda_amps, t2_amps, chol_ov)
        return gathered(lambda_amps, t2_amps, chol_ov)

    placed = (P("pair", "virt", None), P("pair", "virt", None), P("pair", None, "virt"))
    return jax.shard_map(
        shards, mesh=mesh, in_specs=placed, out_specs=P("pair", None, "virt"), check_vma=False
    )
```

```python
import functools

import jax
import jax.numpy as jnp
from jax import lax
from jax.experimental import pallas as pl
from jax.experimental.pallas import tpu as pltpu
from jax.sharding import PartitionSpec as P

AHEAD = 3
PAIR_VMEM = 40 * 2**20
SMALL_VMEM = 12 * 2**20
HBM = pl.BlockSpec(memory_space=pltpu.HBM)
VMEM = pl.BlockSpec(memory_space=pltpu.VMEM)
ANY = pl.BlockSpec(memory_space=pl.ANY)
FREE = pl.CostEstimate(flops=0, bytes_accessed=0, transcendentals=0)


def filler(gigaflops):
    return pl.CostEstimate(flops=int(gigaflops * 10**9), bytes_accessed=0, transcendentals=0)


PLANE_FILL = (filler(5), filler(1))
GROUP_FILL = (filler(2), filler(2))
LAST_FILL = filler(10)


def swap(array, axis, size, offset):
    return lax.ppermute(array, axis, [(i, i ^ offset) for i in range(size)])


def in_vmem(arrays):
    return [pltpu.with_memory_space_constraint(array, pltpu.VMEM) for array in arrays]


def depth_chunks(depth):
    cuts = [0]
    for size in (256, 512, 1024, 1280):
        if cuts[-1] + size < depth:
            cuts.append(cuts[-1] + size)
    while depth - cuts[-1] > 2048:
        cuts.append(cuts[-1] + 1024)
    return [(a, b - a) for a, b in zip(cuts, cuts[1:] + [depth])]


def pair_kernel(chunks, left_hbm, right_hbm, own_hbm, total, own_ref, left, right, sems, own_sem):
    copies = []
    for n, (start, size) in enumerate(chunks):
        span = pl.ds(start, size)
        pair = (
            pltpu.make_async_copy(left_hbm.at[span], left.at[span], sems.at[0, n]),
            pltpu.make_async_copy(right_hbm.at[span], right.at[span], sems.at[1, n]),
        )
        copies.append(pair)
    own_copy = pltpu.make_async_copy(own_hbm, own_ref, own_sem)
    copies.append((own_copy,))
    for copy in [copy for pair in copies[:AHEAD] for copy in pair]:
        copy.start()
    for n, (start, size) in enumerate(chunks):
        for copy in copies[n]:
            copy.wait()
        for copy in [copy for pair in copies[n + AHEAD : n + AHEAD + 1] for copy in pair]:
            copy.start()
        span = pl.ds(start, size)
        term = lax.dot_general(
            left[span], right[span], (((0,), (0,)), ((), ())), preferred_element_type=jnp.float32
        )
        if n == 0:
            total[...] = term
        else:
            total[...] += term
    own_copy.wait()


def pair_product(left, right, own):
    depth, full = left.shape
    chunks = depth_chunks(depth)
    return pl.pallas_call(
        functools.partial(pair_kernel, chunks),
        out_shape=[pltpu.VMEM((full, full), jnp.float32), pltpu.VMEM(own.shape, own.dtype)],
        in_specs=[HBM] * 3,
        out_specs=[VMEM] * 2,
        scratch_shapes=[
            pltpu.VMEM((depth, full), left.dtype),
            pltpu.VMEM((depth, full), right.dtype),
            pltpu.SemaphoreType.DMA((2, len(chunks))),
            pltpu.SemaphoreType.DMA,
        ],
        compiler_params=pltpu.CompilerParams(vmem_limit_bytes=PAIR_VMEM),
        cost_estimate=pl.CostEstimate(
            flops=2 * depth * full * full, bytes_accessed=4 * depth * full, transcendentals=0
        ),
    )(*[pltpu.with_memory_space_constraint(side, pltpu.HBM) for side in (left, right, own)])


def cut_kernel(rows, parity, total, *outs):
    me = lax.axis_index("virt")
    chips = outs[0].shape[0]
    for mine in range(2 * chips):

        @pl.when(me == mine)
        def _():
            core = (mine & 1) ^ parity
            for side, out in enumerate(outs):
                for k in range(chips):
                    chip = (mine >> 1) ^ k
                    first = (2 * chip + (side ^ core)) * rows
                    pieces = []
                    for a in (first, first + rows // 2):
                        for offset in range(chips):
                            b = (2 * (chip ^ offset) + core) * rows
                            pieces.append(total[a : a + rows // 2, b : b + rows])
                    out[k] = jnp.concatenate(pieces, axis=1).astype(out.dtype)


def cut(total, rows, parity, kind):
    full = total.shape[0]
    chips = full // rows // 2
    return pl.pallas_call(
        functools.partial(cut_kernel, rows, parity),
        out_shape=[pltpu.VMEM((chips, rows // 2, full), kind)] * 2,
        in_specs=[VMEM],
        out_specs=[VMEM] * 2,
        compiler_params=pltpu.CompilerParams(vmem_limit_bytes=SMALL_VMEM),
        cost_estimate=FREE,
    )(*in_vmem([total]))


def merge_kernel(sent, rest, count, term, other, *refs):
    narrow, wide = refs[count:]
    for places, out in ((sent, narrow), (rest, wide)):
        for n, k in enumerate(places):
            out[n] = (term[k] + other[k].astype(jnp.float32)).astype(out.dtype)


def merge(term, other, sent, rest, after, cost):
    shape = term.shape[1:]
    return pl.pallas_call(
        functools.partial(merge_kernel, sent, rest, len(after)),
        out_shape=[
            pltpu.VMEM((len(sent), *shape), jnp.bfloat16),
            pltpu.VMEM((len(rest), *shape), jnp.float32),
        ],
        in_specs=[VMEM] * 2 + [ANY] * len(after),
        out_specs=[VMEM] * 2,
        compiler_params=pltpu.CompilerParams(vmem_limit_bytes=SMALL_VMEM),
        cost_estimate=cost,
    )(*in_vmem([term, other]), *after)


def low_kernel(count, vv_ref, part_ref, *refs):
    low_ref = refs[count]
    whole = vv_ref[0] + part_ref[0].astype(jnp.float32)
    half = whole.shape[1] // 2
    low_ref[...] = jnp.concatenate([whole[:, :half], whole[:, half:]], axis=0).astype(low_ref.dtype)


def low_rows(vv, part, after, cost):
    _, rows, full = vv.shape
    return pl.pallas_call(
        functools.partial(low_kernel, len(after)),
        out_shape=pltpu.VMEM((2 * rows, full // 2), jnp.bfloat16),
        in_specs=[VMEM] * 2 + [ANY] * len(after),
        out_specs=VMEM,
        compiler_params=pltpu.CompilerParams(vmem_limit_bytes=SMALL_VMEM),
        cost_estimate=cost,
    )(*in_vmem([vv, part]), *after)


def block_rows(blocks, place):
    return jnp.concatenate([blocks[n][at] for n, at in place], axis=0)


def places_of(blocks):
    arrays = {id(array): array for block in blocks for array, _ in block}
    index = {name: n for n, name in enumerate(arrays)}
    return list(arrays.values()), [[(index[id(array)], at) for array, at in block] for block in blocks]


def other_kernel(places, low_ref, *refs):
    *blocks, out_ref = refs
    for i, place in enumerate(places):
        out_ref[i] = jnp.dot(
            low_ref[...], block_rows(blocks, place), preferred_element_type=jnp.float32
        ).astype(out_ref.dtype)


def other_density(low, blocks):
    arrays, places = places_of(blocks)
    return pl.pallas_call(
        functools.partial(other_kernel, places),
        out_shape=pltpu.VMEM((len(blocks), low.shape[0], arrays[0].shape[2]), jnp.bfloat16),
        in_specs=[VMEM] * (1 + len(arrays)),
        out_specs=VMEM,
        compiler_params=pltpu.CompilerParams(vmem_limit_bytes=SMALL_VMEM),
        cost_estimate=FREE,
    )(*in_vmem([low, *arrays]))


def own_kernel(places, start, low_ref, arrived_ref, *refs):
    out_hbm, out, sems = refs[-3:]
    copies = []
    for i, place in enumerate(places):
        both = jnp.dot(low_ref[...], block_rows(refs, place), preferred_element_type=jnp.float32)
        out[i] = (both + arrived_ref[i].astype(jnp.float32)).astype(out.dtype)
        copies.append(pltpu.make_async_copy(out.at[i], out_hbm.at[start + i], sems.at[i]))
        copies[i].start()
    for copy in copies:
        copy.wait()


def own_density(low, blocks, arrived, start, occ, base):
    arrays, places = places_of(blocks)
    rows, vectors = low.shape[0], arrays[0].shape[2]
    given = [] if base is None else [base]
    return pl.pallas_call(
        functools.partial(own_kernel, places, start),
        out_shape=jax.ShapeDtypeStruct((occ, rows, vectors), jnp.bfloat16),
        in_specs=[VMEM] * (2 + len(arrays)) + [HBM] * len(given),
        out_specs=HBM,
        scratch_shapes=[
            pltpu.VMEM((len(blocks), rows, vectors), jnp.bfloat16),
            pltpu.SemaphoreType.DMA((len(blocks),)),
        ],
        input_output_aliases={2 + len(arrays): 0} if given else {},
        compiler_params=pltpu.CompilerParams(vmem_limit_bytes=SMALL_VMEM),
        cost_estimate=FREE,
    )(*in_vmem([low, arrived, *arrays]), *given)


def load_kernel(cuts, own_hbm, *refs):
    outs, sems = refs[:-1], refs[-1]
    copies = [
        pltpu.make_async_copy(own_hbm.at[pl.ds(start, size)], out, sems.at[n])
        for n, ((start, size), out) in enumerate(zip(cuts, outs))
    ]
    for copy in copies:
        copy.start()
    for copy in copies:
        copy.wait()


def load(own, cuts):
    return pl.pallas_call(
        functools.partial(load_kernel, cuts),
        out_shape=[pltpu.VMEM((size, *own.shape[1:]), own.dtype) for _, size in cuts],
        in_specs=[HBM],
        out_specs=[VMEM] * len(cuts),
        scratch_shapes=[pltpu.SemaphoreType.DMA((len(cuts),))],
        compiler_params=pltpu.CompilerParams(vmem_limit_bytes=SMALL_VMEM),
        cost_estimate=FREE,
    )(pltpu.with_memory_space_constraint(own, pltpu.HBM))


def lay(*arrays):
    return [(array, at) for array in arrays for at in range(array.shape[0])]


def pick(places):
    runs = []
    for array, at in places:
        if runs and runs[-1][0] is array and runs[-1][2] == at:
            runs[-1][2] = at + 1
        else:
            runs.append([array, at, at + 1])
    pieces = [array[start:stop] for array, start, stop in runs]
    return pieces[0] if len(pieces) == 1 else jnp.concatenate(pieces, axis=0)


def permuted(count, groups, lambda_amps, t2_amps, chol_ov):
    rows, full = chol_ov.shape[2], lambda_amps.shape[2]
    own = jnp.transpose(chol_ov, (1, 2, 0))
    occ = own.shape[0]
    half = occ // 2
    bits = [k for k in range(2, count) if k & (k - 1) == 0]
    even = range(0, count, 2)
    early = occ - occ // 4
    first = {k: (0, occ) if k == 2 else (0, early) for k in bits}
    pieces = sorted({cut for cut in first.values() if cut[1] < occ})
    loaded = dict(zip(pieces, load(own, pieces))) if pieces else {}
    came = {k: swap(loaded.get(first[k], own), "virt", count, k) for k in bits}

    product, own = pair_product(lambda_amps.reshape(-1, full), t2_amps.reshape(-1, full), own)
    other = [swap(part, "virt", count, 1) for part in cut(product, rows, 1, jnp.bfloat16)]
    vv = list(cut(product, rows, 0, jnp.float32))
    narrow = [None, None]
    for step in range(len(bits) + 1):
        for side in (1, 0):
            held = range(vv[side].shape[0])
            if step < len(bits):
                bit = (bits[::-1] if side else bits)[step]
                place = len(held) // 2 if side else 1
                sent = [k for k in held if k & place]
                rest = [k for k in held if not k & place]
            else:
                sent = rest = [0]
            after = list(came.values()) if (step, side) == (1, 1) else []
            cost = PLANE_FILL[side] if step == len(bits) else FREE
            narrow[side], vv[side] = merge(vv[side], other[side], sent, rest, after, cost)
            if step < len(bits):
                other[side] = swap(narrow[side], "virt", count, bit)

    held = {0: lay(own)}
    for k in bits:
        start, size = first[k]
        parts = [came[k]]
        if start:
            parts.insert(0, swap(own[:start], "virt", count, k))
        if start + size < occ:
            parts.append(swap(own[start + size :], "virt", count, k))
        held[k] = lay(*parts)
    for k in sorted(set(even) - set(held), key=lambda k: (bin(k).count("1"), k)):
        low_bit, high_bit = k & -k, 1 << (k.bit_length() - 1)
        lower = pick(held[k ^ low_bit][:half])
        upper = pick(held[k ^ high_bit][half:])
        held[k] = lay(swap(lower, "virt", count, low_bit), swap(upper, "virt", count, high_bit))
    blocks = [[held[k][i] for k in even] for i in range(occ)]

    step = 1
    while step < groups:
        part = {side: swap(narrow[side], "pair", groups, step) for side in (1, 0)}
        after = [narrow[0]]
        if 2 * step < groups:
            narrow[1], vv[1] = merge(vv[1], part[1], [0], [0], after, GROUP_FILL[1])
            narrow[0], vv[0] = merge(vv[0], part[0], [0], [0], [], GROUP_FILL[0])
        step *= 2
    low = {1: low_rows(vv[1], part[1], after, FREE), 0: low_rows(vv[0], part[0], [], LAST_FILL)}
    cuts = ((0, half), (half, occ))
    arrived = [swap(other_density(low[1], blocks[a:b]), "virt", count, 1) for a, b in cuts]
    density = None
    for (a, b), part in zip(cuts, arrived):
        density = own_density(low[0], blocks[a:b], part, a, occ, density)
    return jnp.transpose(density, (2, 0, 1))


def gathered(lambda_amps, t2_amps, chol_ov):
    vv = lax.dot_general(
        lambda_amps, t2_amps, (((0, 1), (0, 1)), ((), ())), preferred_element_type=jnp.float32
    )
    vv = lax.psum_scatter(vv, "virt", scatter_dimension=0, tiled=True)
    low = lax.psum(vv, "pair").astype(jnp.bfloat16)
    blocks = lax.all_gather(jnp.transpose(chol_ov, (1, 2, 0)), "virt", axis=1, tiled=True)
    density = jnp.einsum("ab,ibq->iaq", low, blocks, preferred_element_type=jnp.float32)
    return jnp.transpose(density, (2, 0, 1)).astype(jnp.bfloat16)


def solution(mesh):
    count, groups = mesh.shape["virt"], mesh.shape["pair"]
    paired = count & (count - 1) == 0 and groups & (groups - 1) == 0 and count > 3 and groups > 1

    def shards(lambda_amps, t2_amps, chol_ov):
        if paired and chol_ov.shape[2] % 16 == 0 and chol_ov.shape[1] > 1:
            return permuted(count, groups, lambda_amps, t2_amps, chol_ov)
        return gathered(lambda_amps, t2_amps, chol_ov)

    placed = (P("pair", "virt", None), P("pair", "virt", None), P("pair", None, "virt"))
    return jax.shard_map(
        shards, mesh=mesh, in_specs=placed, out_specs=P("pair", None, "virt"), check_vma=False
    )
```

```python
import functools

import jax
import jax.numpy as jnp
from jax import lax
from jax.experimental import pallas as pl
from jax.experimental.pallas import tpu as pltpu
from jax.sharding import PartitionSpec as P

AHEAD = 3
PAIR_VMEM = 40 * 2**20
SMALL_VMEM = 12 * 2**20
HBM = pl.BlockSpec(memory_space=pltpu.HBM)
VMEM = pl.BlockSpec(memory_space=pltpu.VMEM)
ANY = pl.BlockSpec(memory_space=pl.ANY)
FREE = pl.CostEstimate(flops=0, bytes_accessed=0, transcendentals=0)


def filler(gigaflops):
    return pl.CostEstimate(flops=int(gigaflops * 10**9), bytes_accessed=0, transcendentals=0)


PLANE_FILL = (filler(5), filler(1))
GROUP_FILL = (filler(1), filler(1))
LAST_FILL = filler(10)


def swap(array, axis, size, offset):
    return lax.ppermute(array, axis, [(i, i ^ offset) for i in range(size)])


def in_vmem(arrays):
    return [pltpu.with_memory_space_constraint(array, pltpu.VMEM) for array in arrays]


def depth_chunks(depth):
    cuts = [0]
    for size in (256, 512, 1024, 1280):
        if cuts[-1] + size < depth:
            cuts.append(cuts[-1] + size)
    while depth - cuts[-1] > 2048:
        cuts.append(cuts[-1] + 1024)
    return [(a, b - a) for a, b in zip(cuts, cuts[1:] + [depth])]


def pair_kernel(chunks, left_hbm, right_hbm, own_hbm, total, own_ref, left, right, sems, own_sem):
    copies = []
    for n, (start, size) in enumerate(chunks):
        span = pl.ds(start, size)
        pair = (
            pltpu.make_async_copy(left_hbm.at[span], left.at[span], sems.at[0, n]),
            pltpu.make_async_copy(right_hbm.at[span], right.at[span], sems.at[1, n]),
        )
        copies.append(pair)
    own_copy = pltpu.make_async_copy(own_hbm, own_ref, own_sem)
    copies.append((own_copy,))
    for copy in [copy for pair in copies[:AHEAD] for copy in pair]:
        copy.start()
    for n, (start, size) in enumerate(chunks):
        for copy in copies[n]:
            copy.wait()
        for copy in [copy for pair in copies[n + AHEAD : n + AHEAD + 1] for copy in pair]:
            copy.start()
        span = pl.ds(start, size)
        term = lax.dot_general(
            left[span], right[span], (((0,), (0,)), ((), ())), preferred_element_type=jnp.float32
        )
        if n == 0:
            total[...] = term
        else:
            total[...] += term
    own_copy.wait()


def pair_product(left, right, own):
    depth, full = left.shape
    chunks = depth_chunks(depth)
    return pl.pallas_call(
        functools.partial(pair_kernel, chunks),
        out_shape=[pltpu.VMEM((full, full), jnp.float32), pltpu.VMEM(own.shape, own.dtype)],
        in_specs=[HBM] * 3,
        out_specs=[VMEM] * 2,
        scratch_shapes=[
            pltpu.VMEM((depth, full), left.dtype),
            pltpu.VMEM((depth, full), right.dtype),
            pltpu.SemaphoreType.DMA((2, len(chunks))),
            pltpu.SemaphoreType.DMA,
        ],
        compiler_params=pltpu.CompilerParams(vmem_limit_bytes=PAIR_VMEM),
        cost_estimate=pl.CostEstimate(
            flops=2 * depth * full * full, bytes_accessed=4 * depth * full, transcendentals=0
        ),
    )(*[pltpu.with_memory_space_constraint(side, pltpu.HBM) for side in (left, right, own)])


def cut_kernel(rows, parity, total, *outs):
    me = lax.axis_index("virt")
    chips = outs[0].shape[0]
    for mine in range(2 * chips):

        @pl.when(me == mine)
        def _():
            core = (mine & 1) ^ parity
            for side, out in enumerate(outs):
                for k in range(chips):
                    chip = (mine >> 1) ^ k
                    first = (2 * chip + (side ^ core)) * rows
                    pieces = []
                    for a in (first, first + rows // 2):
                        for offset in range(chips):
                            b = (2 * (chip ^ offset) + core) * rows
                            pieces.append(total[a : a + rows // 2, b : b + rows])
                    out[k] = jnp.concatenate(pieces, axis=1).astype(out.dtype)


def cut(total, rows, parity, kind):
    full = total.shape[0]
    chips = full // rows // 2
    return pl.pallas_call(
        functools.partial(cut_kernel, rows, parity),
        out_shape=[pltpu.VMEM((chips, rows // 2, full), kind)] * 2,
        in_specs=[VMEM],
        out_specs=[VMEM] * 2,
        compiler_params=pltpu.CompilerParams(vmem_limit_bytes=SMALL_VMEM),
        cost_estimate=FREE,
    )(*in_vmem([total]))


def merge_kernel(sent, rest, count, term, other, *refs):
    narrow, wide = refs[count:]
    for places, out in ((sent, narrow), (rest, wide)):
        for n, k in enumerate(places):
            out[n] = (term[k] + other[k].astype(jnp.float32)).astype(out.dtype)


def merge(term, other, sent, rest, after, cost):
    shape = term.shape[1:]
    return pl.pallas_call(
        functools.partial(merge_kernel, sent, rest, len(after)),
        out_shape=[
            pltpu.VMEM((len(sent), *shape), jnp.bfloat16),
            pltpu.VMEM((len(rest), *shape), jnp.float32),
        ],
        in_specs=[VMEM] * 2 + [ANY] * len(after),
        out_specs=[VMEM] * 2,
        compiler_params=pltpu.CompilerParams(vmem_limit_bytes=SMALL_VMEM),
        cost_estimate=cost,
    )(*in_vmem([term, other]), *after)


def low_kernel(count, vv_ref, part_ref, *refs):
    low_ref = refs[count]
    whole = vv_ref[0] + part_ref[0].astype(jnp.float32)
    half = whole.shape[1] // 2
    low_ref[...] = jnp.concatenate([whole[:, :half], whole[:, half:]], axis=0).astype(low_ref.dtype)


def low_rows(vv, part, after, cost):
    _, rows, full = vv.shape
    return pl.pallas_call(
        functools.partial(low_kernel, len(after)),
        out_shape=pltpu.VMEM((2 * rows, full // 2), jnp.bfloat16),
        in_specs=[VMEM] * 2 + [ANY] * len(after),
        out_specs=VMEM,
        compiler_params=pltpu.CompilerParams(vmem_limit_bytes=SMALL_VMEM),
        cost_estimate=cost,
    )(*in_vmem([vv, part]), *after)


def block_rows(blocks, place):
    return jnp.concatenate([blocks[n][at] for n, at in place], axis=0)


def places_of(blocks):
    arrays = {id(array): array for block in blocks for array, _ in block}
    index = {name: n for n, name in enumerate(arrays)}
    return list(arrays.values()), [[(index[id(array)], at) for array, at in block] for block in blocks]


def other_kernel(places, low_ref, *refs):
    *blocks, out_ref = refs
    for i, place in enumerate(places):
        out_ref[i] = jnp.dot(
            low_ref[...], block_rows(blocks, place), preferred_element_type=jnp.float32
        ).astype(out_ref.dtype)


def other_density(low, blocks):
    arrays, places = places_of(blocks)
    return pl.pallas_call(
        functools.partial(other_kernel, places),
        out_shape=pltpu.VMEM((len(blocks), low.shape[0], arrays[0].shape[2]), jnp.bfloat16),
        in_specs=[VMEM] * (1 + len(arrays)),
        out_specs=VMEM,
        compiler_params=pltpu.CompilerParams(vmem_limit_bytes=SMALL_VMEM),
        cost_estimate=FREE,
    )(*in_vmem([low, *arrays]))


def own_rows(places, low_ref, arrived_ref, blocks, out):
    for i, place in enumerate(places):
        both = jnp.dot(low_ref[...], block_rows(blocks, place), preferred_element_type=jnp.float32)
        out[i] = (both + arrived_ref[i].astype(jnp.float32)).astype(out.dtype)
        yield i


def first_kernel(places, low_ref, arrived_ref, *refs):
    for _ in own_rows(places, low_ref, arrived_ref, refs[:-1], refs[-1]):
        pass


def last_kernel(places, low_ref, arrived_ref, head_ref, *refs):
    *blocks, out_hbm, out, sems = refs
    head = head_ref.shape[0]
    copies = [pltpu.make_async_copy(head_ref, out_hbm.at[pl.ds(0, head)], sems.at[len(places)])]
    copies[0].start()
    for i in own_rows(places, low_ref, arrived_ref, blocks, out):
        copies.append(pltpu.make_async_copy(out.at[i], out_hbm.at[head + i], sems.at[i]))
        copies[-1].start()
    for copy in copies:
        copy.wait()


def own_density(low, blocks, arrived, head):
    arrays, places = places_of(blocks)
    count, rows, vectors = len(blocks), low.shape[0], arrays[0].shape[2]
    given = [] if head is None else [head]
    if head is None:
        kernel, out_spec, scratch = first_kernel, VMEM, []
        out = pltpu.VMEM((count, rows, vectors), jnp.bfloat16)
    else:
        kernel, out_spec = last_kernel, HBM
        out = jax.ShapeDtypeStruct((head.shape[0] + count, rows, vectors), jnp.bfloat16)
        scratch = [
            pltpu.VMEM((count, rows, vectors), jnp.bfloat16),
            pltpu.SemaphoreType.DMA((count + 1,)),
        ]
    return pl.pallas_call(
        functools.partial(kernel, places),
        out_shape=out,
        in_specs=[VMEM] * (2 + len(given) + len(arrays)),
        out_specs=out_spec,
        scratch_shapes=scratch,
        compiler_params=pltpu.CompilerParams(vmem_limit_bytes=SMALL_VMEM),
        cost_estimate=FREE,
    )(*in_vmem([low, arrived, *given, *arrays]))


def lay(*arrays):
    return [(array, at) for array in arrays for at in range(array.shape[0])]


def pick(places):
    runs = []
    for array, at in places:
        if runs and runs[-1][0] is array and runs[-1][2] == at:
            runs[-1][2] = at + 1
        else:
            runs.append([array, at, at + 1])
    pieces = [array[start:stop] for array, start, stop in runs]
    return pieces[0] if len(pieces) == 1 else jnp.concatenate(pieces, axis=0)


def permuted(count, groups, lambda_amps, t2_amps, chol_ov):
    rows, full = chol_ov.shape[2], lambda_amps.shape[2]
    own = jnp.transpose(chol_ov, (1, 2, 0))
    occ = own.shape[0]
    half = occ // 2
    bits = [k for k in range(2, count) if k & (k - 1) == 0]
    even = range(0, count, 2)
    came = {k: swap(own, "virt", count, k) for k in bits}

    product, own = pair_product(lambda_amps.reshape(-1, full), t2_amps.reshape(-1, full), own)
    other = [swap(part, "virt", count, 1) for part in cut(product, rows, 1, jnp.bfloat16)]
    vv = list(cut(product, rows, 0, jnp.float32))
    narrow = [None, None]
    for step in range(len(bits) + 1):
        for side in (1, 0):
            held = range(vv[side].shape[0])
            if step < len(bits):
                bit = (bits if side else bits[::-1])[step]
                place = 1 if side else len(held) // 2
                sent = [k for k in held if k & place]
                rest = [k for k in held if not k & place]
            else:
                sent = rest = [0]
            after = list(came.values()) if (step, side) == (1, 1) else []
            cost = PLANE_FILL[side] if step == len(bits) else FREE
            narrow[side], vv[side] = merge(vv[side], other[side], sent, rest, after, cost)
            if step < len(bits):
                other[side] = swap(narrow[side], "virt", count, bit)

    held = {0: lay(own)} | {k: lay(came[k]) for k in bits}
    for k in sorted(set(even) - set(held), key=lambda k: (bin(k).count("1"), k)):
        low_bit, high_bit = k & -k, 1 << (k.bit_length() - 1)
        lower = pick(held[k ^ low_bit][:half])
        upper = pick(held[k ^ high_bit][half:])
        held[k] = lay(swap(lower, "virt", count, low_bit), swap(upper, "virt", count, high_bit))
    blocks = [[held[k][i] for k in even] for i in range(occ)]

    step = 1
    while step < groups:
        part = {side: swap(narrow[side], "pair", groups, step) for side in (1, 0)}
        after = [narrow[0]]
        if 2 * step < groups:
            narrow[1], vv[1] = merge(vv[1], part[1], [0], [0], after, GROUP_FILL[1])
            narrow[0], vv[0] = merge(vv[0], part[0], [0], [0], [], GROUP_FILL[0])
        step *= 2
    low = {1: low_rows(vv[1], part[1], after, FREE), 0: low_rows(vv[0], part[0], [], LAST_FILL)}
    cuts = ((0, half), (half, occ))
    arrived = [swap(other_density(low[1], blocks[a:b]), "virt", count, 1) for a, b in cuts]
    density = None
    for (a, b), part in zip(cuts, arrived):
        density = own_density(low[0], blocks[a:b], part, density)
    return jnp.transpose(density, (2, 0, 1))


def gathered(lambda_amps, t2_amps, chol_ov):
    vv = lax.dot_general(
        lambda_amps, t2_amps, (((0, 1), (0, 1)), ((), ())), preferred_element_type=jnp.float32
    )
    vv = lax.psum_scatter(vv, "virt", scatter_dimension=0, tiled=True)
    low = lax.psum(vv, "pair").astype(jnp.bfloat16)
    blocks = lax.all_gather(jnp.transpose(chol_ov, (1, 2, 0)), "virt", axis=1, tiled=True)
    density = jnp.einsum("ab,ibq->iaq", low, blocks, preferred_element_type=jnp.float32)
    return jnp.transpose(density, (2, 0, 1)).astype(jnp.bfloat16)


def solution(mesh):
    count, groups = mesh.shape["virt"], mesh.shape["pair"]
    paired = count & (count - 1) == 0 and groups & (groups - 1) == 0 and count > 3 and groups > 1

    def shards(lambda_amps, t2_amps, chol_ov):
        if paired and chol_ov.shape[2] % 16 == 0 and chol_ov.shape[1] > 1:
            return permuted(count, groups, lambda_amps, t2_amps, chol_ov)
        return gathered(lambda_amps, t2_amps, chol_ov)

    placed = (P("pair", "virt", None), P("pair", "virt", None), P("pair", None, "virt"))
    return jax.shard_map(
        shards, mesh=mesh, in_specs=placed, out_specs=P("pair", None, "virt"), check_vma=False
    )
```

```python
import functools

import jax
import jax.numpy as jnp
from jax import lax
from jax.experimental import pallas as pl
from jax.experimental.pallas import tpu as pltpu
from jax.sharding import PartitionSpec as P

AHEAD = 3
PAIR_VMEM = 40 * 2**20
SMALL_VMEM = 12 * 2**20
HBM = pl.BlockSpec(memory_space=pltpu.HBM)
VMEM = pl.BlockSpec(memory_space=pltpu.VMEM)
ANY = pl.BlockSpec(memory_space=pl.ANY)
FREE = pl.CostEstimate(flops=0, bytes_accessed=0, transcendentals=0)


def filler(gigaflops):
    return pl.CostEstimate(flops=int(gigaflops * 10**9), bytes_accessed=0, transcendentals=0)


PLANE_FILL = (filler(5), filler(1))
GROUP_FILL = (filler(1), filler(1))
LAST_FILL = filler(10)


def swap(array, axis, size, offset):
    return lax.ppermute(array, axis, [(i, i ^ offset) for i in range(size)])


def in_vmem(arrays):
    return [pltpu.with_memory_space_constraint(array, pltpu.VMEM) for array in arrays]


def depth_chunks(depth):
    cuts = [0]
    for size in (256, 512, 1024, 1280):
        if cuts[-1] + size < depth:
            cuts.append(cuts[-1] + size)
    while depth - cuts[-1] > 2048:
        cuts.append(cuts[-1] + 1024)
    return [(a, b - a) for a, b in zip(cuts, cuts[1:] + [depth])]


def pair_kernel(chunks, left_hbm, right_hbm, own_hbm, total, own_ref, left, right, sems, own_sem):
    copies = []
    for n, (start, size) in enumerate(chunks):
        span = pl.ds(start, size)
        pair = (
            pltpu.make_async_copy(left_hbm.at[span], left.at[span], sems.at[0, n]),
            pltpu.make_async_copy(right_hbm.at[span], right.at[span], sems.at[1, n]),
        )
        copies.append(pair)
    own_copy = pltpu.make_async_copy(own_hbm, own_ref, own_sem)
    copies.append((own_copy,))
    for copy in [copy for pair in copies[:AHEAD] for copy in pair]:
        copy.start()
    for n, (start, size) in enumerate(chunks):
        for copy in copies[n]:
            copy.wait()
        for copy in [copy for pair in copies[n + AHEAD : n + AHEAD + 1] for copy in pair]:
            copy.start()
        span = pl.ds(start, size)
        term = lax.dot_general(
            left[span], right[span], (((0,), (0,)), ((), ())), preferred_element_type=jnp.float32
        )
        if n == 0:
            total[...] = term
        else:
            total[...] += term
    own_copy.wait()


def pair_product(left, right, own):
    depth, full = left.shape
    chunks = depth_chunks(depth)
    return pl.pallas_call(
        functools.partial(pair_kernel, chunks),
        out_shape=[pltpu.VMEM((full, full), jnp.float32), pltpu.VMEM(own.shape, own.dtype)],
        in_specs=[HBM] * 3,
        out_specs=[VMEM] * 2,
        scratch_shapes=[
            pltpu.VMEM((depth, full), left.dtype),
            pltpu.VMEM((depth, full), right.dtype),
            pltpu.SemaphoreType.DMA((2, len(chunks))),
            pltpu.SemaphoreType.DMA,
        ],
        compiler_params=pltpu.CompilerParams(vmem_limit_bytes=PAIR_VMEM),
        cost_estimate=pl.CostEstimate(
            flops=2 * depth * full * full, bytes_accessed=4 * depth * full, transcendentals=0
        ),
    )(*[pltpu.with_memory_space_constraint(side, pltpu.HBM) for side in (left, right, own)])


def cut_kernel(rows, parity, total, *outs):
    me = lax.axis_index("virt")
    chips = outs[0].shape[0]
    for mine in range(2 * chips):

        @pl.when(me == mine)
        def _():
            core = (mine & 1) ^ parity
            for side, out in enumerate(outs):
                for k in range(chips):
                    chip = (mine >> 1) ^ k
                    first = (2 * chip + (side ^ core)) * rows
                    pieces = []
                    for a in (first, first + rows // 2):
                        for offset in range(chips):
                            b = (2 * (chip ^ offset) + core) * rows
                            pieces.append(total[a : a + rows // 2, b : b + rows])
                    out[k] = jnp.concatenate(pieces, axis=1).astype(out.dtype)


def cut(total, rows, parity, kind):
    full = total.shape[0]
    chips = full // rows // 2
    return pl.pallas_call(
        functools.partial(cut_kernel, rows, parity),
        out_shape=[pltpu.VMEM((chips, rows // 2, full), kind)] * 2,
        in_specs=[VMEM],
        out_specs=[VMEM] * 2,
        compiler_params=pltpu.CompilerParams(vmem_limit_bytes=SMALL_VMEM),
        cost_estimate=FREE,
    )(*in_vmem([total]))


def merge_kernel(sent, rest, count, term, other, *refs):
    narrow, wide = refs[count:]
    for places, out in ((sent, narrow), (rest, wide)):
        for n, k in enumerate(places):
            out[n] = (term[k] + other[k].astype(jnp.float32)).astype(out.dtype)


def merge(term, other, sent, rest, after, cost):
    shape = term.shape[1:]
    return pl.pallas_call(
        functools.partial(merge_kernel, sent, rest, len(after)),
        out_shape=[
            pltpu.VMEM((len(sent), *shape), jnp.bfloat16),
            pltpu.VMEM((len(rest), *shape), jnp.float32),
        ],
        in_specs=[VMEM] * 2 + [ANY] * len(after),
        out_specs=[VMEM] * 2,
        compiler_params=pltpu.CompilerParams(vmem_limit_bytes=SMALL_VMEM),
        cost_estimate=cost,
    )(*in_vmem([term, other]), *after)


def low_kernel(count, vv_ref, part_ref, *refs):
    low_ref = refs[count]
    whole = vv_ref[0] + part_ref[0].astype(jnp.float32)
    half = whole.shape[1] // 2
    low_ref[...] = jnp.concatenate([whole[:, :half], whole[:, half:]], axis=0).astype(low_ref.dtype)


def low_rows(vv, part, after, cost):
    _, rows, full = vv.shape
    return pl.pallas_call(
        functools.partial(low_kernel, len(after)),
        out_shape=pltpu.VMEM((2 * rows, full // 2), jnp.bfloat16),
        in_specs=[VMEM] * 2 + [ANY] * len(after),
        out_specs=VMEM,
        compiler_params=pltpu.CompilerParams(vmem_limit_bytes=SMALL_VMEM),
        cost_estimate=cost,
    )(*in_vmem([vv, part]), *after)


def block_rows(blocks, place):
    return jnp.concatenate([blocks[n][at] for n, at in place], axis=0)


def places_of(blocks):
    arrays = {id(array): array for block in blocks for array, _ in block}
    index = {name: n for n, name in enumerate(arrays)}
    return list(arrays.values()), [[(index[id(array)], at) for array, at in block] for block in blocks]


def other_kernel(places, low_ref, *refs):
    *blocks, out_ref = refs
    for i, place in enumerate(places):
        out_ref[i] = jnp.dot(
            low_ref[...], block_rows(blocks, place), preferred_element_type=jnp.float32
        ).astype(out_ref.dtype)


def other_density(low, blocks):
    arrays, places = places_of(blocks)
    return pl.pallas_call(
        functools.partial(other_kernel, places),
        out_shape=pltpu.VMEM((len(blocks), low.shape[0], arrays[0].shape[2]), jnp.bfloat16),
        in_specs=[VMEM] * (1 + len(arrays)),
        out_specs=VMEM,
        compiler_params=pltpu.CompilerParams(vmem_limit_bytes=SMALL_VMEM),
        cost_estimate=FREE,
    )(*in_vmem([low, *arrays]))


def own_rows(places, low_ref, arrived_ref, blocks, out):
    for i, place in enumerate(places):
        both = jnp.dot(low_ref[...], block_rows(blocks, place), preferred_element_type=jnp.float32)
        out[i] = (both + arrived_ref[i].astype(jnp.float32)).astype(out.dtype)
        yield i


def first_kernel(places, low_ref, arrived_ref, *refs):
    for _ in own_rows(places, low_ref, arrived_ref, refs[:-1], refs[-1]):
        pass


def last_kernel(places, count, low_ref, arrived_ref, *refs):
    heads, blocks = refs[:count], refs[count:-3]
    out_hbm, out, sems = refs[-3:]
    copies, at = [], 0
    for n, head in enumerate(heads):
        span = pl.ds(at, head.shape[0])
        copies.append(pltpu.make_async_copy(head, out_hbm.at[span], sems.at[len(places) + n]))
        copies[-1].start()
        at += head.shape[0]
    for i in own_rows(places, low_ref, arrived_ref, blocks, out):
        copies.append(pltpu.make_async_copy(out.at[i], out_hbm.at[at + i], sems.at[i]))
        copies[-1].start()
    for copy in copies:
        copy.wait()


def own_density(low, blocks, arrived, heads):
    arrays, places = places_of(blocks)
    count, rows, vectors = len(blocks), low.shape[0], arrays[0].shape[2]
    given = heads or []
    if heads is None:
        kernel, out_spec, scratch = functools.partial(first_kernel, places), VMEM, []
        out = pltpu.VMEM((count, rows, vectors), jnp.bfloat16)
    else:
        kernel, out_spec = functools.partial(last_kernel, places, len(given)), HBM
        occ = sum(head.shape[0] for head in given) + count
        out = jax.ShapeDtypeStruct((occ, rows, vectors), jnp.bfloat16)
        scratch = [
            pltpu.VMEM((count, rows, vectors), jnp.bfloat16),
            pltpu.SemaphoreType.DMA((count + len(given),)),
        ]
    return pl.pallas_call(
        kernel,
        out_shape=out,
        in_specs=[VMEM] * (2 + len(given) + len(arrays)),
        out_specs=out_spec,
        scratch_shapes=scratch,
        compiler_params=pltpu.CompilerParams(vmem_limit_bytes=SMALL_VMEM),
        cost_estimate=FREE,
    )(*in_vmem([low, arrived, *given, *arrays]))


def lay(*arrays):
    return [(array, at) for array in arrays for at in range(array.shape[0])]


def pick(places):
    runs = []
    for array, at in places:
        if runs and runs[-1][0] is array and runs[-1][2] == at:
            runs[-1][2] = at + 1
        else:
            runs.append([array, at, at + 1])
    pieces = [array[start:stop] for array, start, stop in runs]
    return pieces[0] if len(pieces) == 1 else jnp.concatenate(pieces, axis=0)


def permuted(count, groups, lambda_amps, t2_amps, chol_ov):
    rows, full = chol_ov.shape[2], lambda_amps.shape[2]
    own = jnp.transpose(chol_ov, (1, 2, 0))
    occ = own.shape[0]
    half = occ // 2
    bits = [k for k in range(2, count) if k & (k - 1) == 0]
    even = range(0, count, 2)
    came = {k: swap(own, "virt", count, k) for k in bits}

    product, own = pair_product(lambda_amps.reshape(-1, full), t2_amps.reshape(-1, full), own)
    other = [swap(part, "virt", count, 1) for part in cut(product, rows, 1, jnp.bfloat16)]
    vv = list(cut(product, rows, 0, jnp.float32))
    narrow = [None, None]
    for step in range(len(bits) + 1):
        for side in (1, 0):
            held = range(vv[side].shape[0])
            if step < len(bits):
                bit = (bits if side else bits[::-1])[step]
                place = 1 if side else len(held) // 2
                sent = [k for k in held if k & place]
                rest = [k for k in held if not k & place]
            else:
                sent = rest = [0]
            after = list(came.values()) if (step, side) == (1, 1) else []
            cost = PLANE_FILL[side] if step == len(bits) else FREE
            narrow[side], vv[side] = merge(vv[side], other[side], sent, rest, after, cost)
            if step < len(bits):
                other[side] = swap(narrow[side], "virt", count, bit)

    held = {0: lay(own)} | {k: lay(came[k]) for k in bits}
    for k in sorted(set(even) - set(held), key=lambda k: (bin(k).count("1"), k)):
        low_bit, high_bit = k & -k, 1 << (k.bit_length() - 1)
        lower = pick(held[k ^ low_bit][:half])
        upper = pick(held[k ^ high_bit][half:])
        held[k] = lay(swap(lower, "virt", count, low_bit), swap(upper, "virt", count, high_bit))
    blocks = [[held[k][i] for k in even] for i in range(occ)]

    step = 1
    while step < groups:
        part = {side: swap(narrow[side], "pair", groups, step) for side in (1, 0)}
        after = [narrow[0]]
        if 2 * step < groups:
            narrow[1], vv[1] = merge(vv[1], part[1], [0], [0], after, GROUP_FILL[1])
            narrow[0], vv[0] = merge(vv[0], part[0], [0], [0], [], GROUP_FILL[0])
        step *= 2
    low = {1: low_rows(vv[1], part[1], after, FREE), 0: low_rows(vv[0], part[0], [], LAST_FILL)}
    edges = sorted({0, occ - 1, occ})
    cuts = list(zip(edges, edges[1:]))
    arrived = [swap(other_density(low[1], blocks[a:b]), "virt", count, 1) for a, b in cuts]
    heads = [
        own_density(low[0], blocks[a:b], part, None) for (a, b), part in zip(cuts[:-1], arrived)
    ]
    density = own_density(low[0], blocks[cuts[-1][0] :], arrived[-1], heads)
    return jnp.transpose(density, (2, 0, 1))


def gathered(lambda_amps, t2_amps, chol_ov):
    vv = lax.dot_general(
        lambda_amps, t2_amps, (((0, 1), (0, 1)), ((), ())), preferred_element_type=jnp.float32
    )
    vv = lax.psum_scatter(vv, "virt", scatter_dimension=0, tiled=True)
    low = lax.psum(vv, "pair").astype(jnp.bfloat16)
    blocks = lax.all_gather(jnp.transpose(chol_ov, (1, 2, 0)), "virt", axis=1, tiled=True)
    density = jnp.einsum("ab,ibq->iaq", low, blocks, preferred_element_type=jnp.float32)
    return jnp.transpose(density, (2, 0, 1)).astype(jnp.bfloat16)


def solution(mesh):
    count, groups = mesh.shape["virt"], mesh.shape["pair"]
    paired = count & (count - 1) == 0 and groups & (groups - 1) == 0 and count > 3 and groups > 1

    def shards(lambda_amps, t2_amps, chol_ov):
        if paired and chol_ov.shape[2] % 16 == 0 and chol_ov.shape[1] > 1:
            return permuted(count, groups, lambda_amps, t2_amps, chol_ov)
        return gathered(lambda_amps, t2_amps, chol_ov)

    placed = (P("pair", "virt", None), P("pair", "virt", None), P("pair", None, "virt"))
    return jax.shard_map(
        shards, mesh=mesh, in_specs=placed, out_specs=P("pair", None, "virt"), check_vma=False
    )
```

```python
import functools

import jax
import jax.numpy as jnp
from jax import lax
from jax.experimental import pallas as pl
from jax.experimental.pallas import tpu as pltpu
from jax.sharding import PartitionSpec as P

AHEAD = 3
PAIR_VMEM = 40 * 2**20
SMALL_VMEM = 12 * 2**20
HBM = pl.BlockSpec(memory_space=pltpu.HBM)
VMEM = pl.BlockSpec(memory_space=pltpu.VMEM)
ANY = pl.BlockSpec(memory_space=pl.ANY)
FREE = pl.CostEstimate(flops=0, bytes_accessed=0, transcendentals=0)


def filler(gigaflops):
    return pl.CostEstimate(flops=int(gigaflops * 10**9), bytes_accessed=0, transcendentals=0)


PLANE_FILL = (filler(5), filler(1))
GROUP_FILL = (filler(0.5), filler(1))
LAST_FILL = filler(10)


def swap(array, axis, size, offset):
    return lax.ppermute(array, axis, [(i, i ^ offset) for i in range(size)])


def in_vmem(arrays):
    return [pltpu.with_memory_space_constraint(array, pltpu.VMEM) for array in arrays]


def depth_chunks(depth):
    cuts = [0]
    for size in (256, 512, 1024, 1280):
        if cuts[-1] + size < depth:
            cuts.append(cuts[-1] + size)
    while depth - cuts[-1] > 2048:
        cuts.append(cuts[-1] + 1024)
    return [(a, b - a) for a, b in zip(cuts, cuts[1:] + [depth])]


def pair_kernel(chunks, left_hbm, right_hbm, own_hbm, total, own_ref, left, right, sems, own_sem):
    copies = []
    for n, (start, size) in enumerate(chunks):
        span = pl.ds(start, size)
        pair = (
            pltpu.make_async_copy(left_hbm.at[span], left.at[span], sems.at[0, n]),
            pltpu.make_async_copy(right_hbm.at[span], right.at[span], sems.at[1, n]),
        )
        copies.append(pair)
    own_copy = pltpu.make_async_copy(own_hbm, own_ref, own_sem)
    copies.append((own_copy,))
    for copy in [copy for pair in copies[:AHEAD] for copy in pair]:
        copy.start()
    for n, (start, size) in enumerate(chunks):
        for copy in copies[n]:
            copy.wait()
        for copy in [copy for pair in copies[n + AHEAD : n + AHEAD + 1] for copy in pair]:
            copy.start()
        span = pl.ds(start, size)
        term = lax.dot_general(
            left[span], right[span], (((0,), (0,)), ((), ())), preferred_element_type=jnp.float32
        )
        if n == 0:
            total[...] = term
        else:
            total[...] += term
    own_copy.wait()


def pair_product(left, right, own):
    depth, full = left.shape
    chunks = depth_chunks(depth)
    return pl.pallas_call(
        functools.partial(pair_kernel, chunks),
        out_shape=[pltpu.VMEM((full, full), jnp.float32), pltpu.VMEM(own.shape, own.dtype)],
        in_specs=[HBM] * 3,
        out_specs=[VMEM] * 2,
        scratch_shapes=[
            pltpu.VMEM((depth, full), left.dtype),
            pltpu.VMEM((depth, full), right.dtype),
            pltpu.SemaphoreType.DMA((2, len(chunks))),
            pltpu.SemaphoreType.DMA,
        ],
        compiler_params=pltpu.CompilerParams(vmem_limit_bytes=PAIR_VMEM),
        cost_estimate=pl.CostEstimate(
            flops=2 * depth * full * full, bytes_accessed=4 * depth * full, transcendentals=0
        ),
    )(*[pltpu.with_memory_space_constraint(side, pltpu.HBM) for side in (left, right, own)])


def cut_kernel(rows, parity, total, *outs):
    me = lax.axis_index("virt")
    chips = outs[0].shape[0]
    for mine in range(2 * chips):

        @pl.when(me == mine)
        def _():
            core = (mine & 1) ^ parity
            for side, out in enumerate(outs):
                for k in range(chips):
                    chip = (mine >> 1) ^ k
                    first = (2 * chip + (side ^ core)) * rows
                    pieces = []
                    for a in (first, first + rows // 2):
                        for offset in range(chips):
                            b = (2 * (chip ^ offset) + core) * rows
                            pieces.append(total[a : a + rows // 2, b : b + rows])
                    out[k] = jnp.concatenate(pieces, axis=1).astype(out.dtype)


def cut(total, rows, parity, kind):
    full = total.shape[0]
    chips = full // rows // 2
    return pl.pallas_call(
        functools.partial(cut_kernel, rows, parity),
        out_shape=[pltpu.VMEM((chips, rows // 2, full), kind)] * 2,
        in_specs=[VMEM],
        out_specs=[VMEM] * 2,
        compiler_params=pltpu.CompilerParams(vmem_limit_bytes=SMALL_VMEM),
        cost_estimate=FREE,
    )(*in_vmem([total]))


def merge_kernel(sent, rest, count, term, other, *refs):
    narrow, wide = refs[count:]
    for places, out in ((sent, narrow), (rest, wide)):
        for n, k in enumerate(places):
            out[n] = (term[k] + other[k].astype(jnp.float32)).astype(out.dtype)


def merge(term, other, sent, rest, after, cost):
    shape = term.shape[1:]
    return pl.pallas_call(
        functools.partial(merge_kernel, sent, rest, len(after)),
        out_shape=[
            pltpu.VMEM((len(sent), *shape), jnp.bfloat16),
            pltpu.VMEM((len(rest), *shape), jnp.float32),
        ],
        in_specs=[VMEM] * 2 + [ANY] * len(after),
        out_specs=[VMEM] * 2,
        compiler_params=pltpu.CompilerParams(vmem_limit_bytes=SMALL_VMEM),
        cost_estimate=cost,
    )(*in_vmem([term, other]), *after)


def low_kernel(count, vv_ref, part_ref, *refs):
    low_ref = refs[count]
    whole = vv_ref[0] + part_ref[0].astype(jnp.float32)
    half = whole.shape[1] // 2
    low_ref[...] = jnp.concatenate([whole[:, :half], whole[:, half:]], axis=0).astype(low_ref.dtype)


def low_rows(vv, part, after, cost):
    _, rows, full = vv.shape
    return pl.pallas_call(
        functools.partial(low_kernel, len(after)),
        out_shape=pltpu.VMEM((2 * rows, full // 2), jnp.bfloat16),
        in_specs=[VMEM] * 2 + [ANY] * len(after),
        out_specs=VMEM,
        compiler_params=pltpu.CompilerParams(vmem_limit_bytes=SMALL_VMEM),
        cost_estimate=cost,
    )(*in_vmem([vv, part]), *after)


def block_rows(blocks, place):
    return jnp.concatenate([blocks[n][at] for n, at in place], axis=0)


def places_of(blocks):
    arrays = {id(array): array for block in blocks for array, _ in block}
    index = {name: n for n, name in enumerate(arrays)}
    return list(arrays.values()), [[(index[id(array)], at) for array, at in block] for block in blocks]


def other_kernel(places, low_ref, *refs):
    *blocks, out_ref = refs
    for i, place in enumerate(places):
        out_ref[i] = jnp.dot(
            low_ref[...], block_rows(blocks, place), preferred_element_type=jnp.float32
        ).astype(out_ref.dtype)


def other_density(low, blocks):
    arrays, places = places_of(blocks)
    return pl.pallas_call(
        functools.partial(other_kernel, places),
        out_shape=pltpu.VMEM((len(blocks), low.shape[0], arrays[0].shape[2]), jnp.bfloat16),
        in_specs=[VMEM] * (1 + len(arrays)),
        out_specs=VMEM,
        compiler_params=pltpu.CompilerParams(vmem_limit_bytes=SMALL_VMEM),
        cost_estimate=FREE,
    )(*in_vmem([low, *arrays]))


def own_rows(places, low_ref, arrived_ref, blocks, out):
    for i, place in enumerate(places):
        both = jnp.dot(low_ref[...], block_rows(blocks, place), preferred_element_type=jnp.float32)
        out[i] = (both + arrived_ref[i].astype(jnp.float32)).astype(out.dtype)
        yield i


def first_kernel(places, low_ref, arrived_ref, *refs):
    for _ in own_rows(places, low_ref, arrived_ref, refs[:-1], refs[-1]):
        pass


def last_kernel(places, low_ref, arrived_ref, head_ref, *refs):
    *blocks, out_hbm, out, sems = refs
    head = head_ref.shape[0]
    copies = [pltpu.make_async_copy(head_ref, out_hbm.at[pl.ds(0, head)], sems.at[len(places)])]
    copies[0].start()
    for i in own_rows(places, low_ref, arrived_ref, blocks, out):
        copies.append(pltpu.make_async_copy(out.at[i], out_hbm.at[head + i], sems.at[i]))
        copies[-1].start()
    for copy in copies:
        copy.wait()


def own_density(low, blocks, arrived, head):
    arrays, places = places_of(blocks)
    count, rows, vectors = len(blocks), low.shape[0], arrays[0].shape[2]
    given = [] if head is None else [head]
    if head is None:
        kernel, out_spec, scratch = first_kernel, VMEM, []
        out = pltpu.VMEM((count, rows, vectors), jnp.bfloat16)
    else:
        kernel, out_spec = last_kernel, HBM
        out = jax.ShapeDtypeStruct((head.shape[0] + count, rows, vectors), jnp.bfloat16)
        scratch = [
            pltpu.VMEM((count, rows, vectors), jnp.bfloat16),
            pltpu.SemaphoreType.DMA((count + 1,)),
        ]
    return pl.pallas_call(
        functools.partial(kernel, places),
        out_shape=out,
        in_specs=[VMEM] * (2 + len(given) + len(arrays)),
        out_specs=out_spec,
        scratch_shapes=scratch,
        compiler_params=pltpu.CompilerParams(vmem_limit_bytes=SMALL_VMEM),
        cost_estimate=FREE,
    )(*in_vmem([low, arrived, *given, *arrays]))


def lay(*arrays):
    return [(array, at) for array in arrays for at in range(array.shape[0])]


def pick(places):
    runs = []
    for array, at in places:
        if runs and runs[-1][0] is array and runs[-1][2] == at:
            runs[-1][2] = at + 1
        else:
            runs.append([array, at, at + 1])
    pieces = [array[start:stop] for array, start, stop in runs]
    return pieces[0] if len(pieces) == 1 else jnp.concatenate(pieces, axis=0)


def permuted(count, groups, lambda_amps, t2_amps, chol_ov):
    rows, full = chol_ov.shape[2], lambda_amps.shape[2]
    own = jnp.transpose(chol_ov, (1, 2, 0))
    occ = own.shape[0]
    half = occ // 2
    bits = [k for k in range(2, count) if k & (k - 1) == 0]
    even = range(0, count, 2)
    came = {k: swap(own, "virt", count, k) for k in bits}

    product, own = pair_product(lambda_amps.reshape(-1, full), t2_amps.reshape(-1, full), own)
    other = [swap(part, "virt", count, 1) for part in cut(product, rows, 1, jnp.bfloat16)]
    vv = list(cut(product, rows, 0, jnp.float32))
    narrow = [None, None]
    for step in range(len(bits) + 1):
        for side in (1, 0):
            held = range(vv[side].shape[0])
            if step < len(bits):
                bit = (bits if side else bits[::-1])[step]
                place = 1 if side else len(held) // 2
                sent = [k for k in held if k & place]
                rest = [k for k in held if not k & place]
            else:
                sent = rest = [0]
            after = list(came.values()) if (step, side) == (1, 1) else []
            cost = PLANE_FILL[side] if step == len(bits) else FREE
            narrow[side], vv[side] = merge(vv[side], other[side], sent, rest, after, cost)
            if step < len(bits):
                other[side] = swap(narrow[side], "virt", count, bit)

    held = {0: lay(own)} | {k: lay(came[k]) for k in bits}
    for k in sorted(set(even) - set(held), key=lambda k: (bin(k).count("1"), k)):
        low_bit, high_bit = k & -k, 1 << (k.bit_length() - 1)
        lower = pick(held[k ^ low_bit][:half])
        upper = pick(held[k ^ high_bit][half:])
        held[k] = lay(swap(lower, "virt", count, low_bit), swap(upper, "virt", count, high_bit))
    blocks = [[held[k][i] for k in even] for i in range(occ)]

    step = 1
    while step < groups:
        part = {side: swap(narrow[side], "pair", groups, step) for side in (1, 0)}
        after = [narrow[0]]
        if 2 * step < groups:
            narrow[1], vv[1] = merge(vv[1], part[1], [0], [0], after, GROUP_FILL[1])
            narrow[0], vv[0] = merge(vv[0], part[0], [0], [0], [], GROUP_FILL[0])
        step *= 2
    low = {1: low_rows(vv[1], part[1], after, FREE), 0: low_rows(vv[0], part[0], [], LAST_FILL)}
    cuts = ((0, half), (half, occ))
    arrived = [swap(other_density(low[1], blocks[a:b]), "virt", count, 1) for a, b in cuts]
    density = None
    for (a, b), part in zip(cuts, arrived):
        density = own_density(low[0], blocks[a:b], part, density)
    return jnp.transpose(density, (2, 0, 1))


def gathered(lambda_amps, t2_amps, chol_ov):
    vv = lax.dot_general(
        lambda_amps, t2_amps, (((0, 1), (0, 1)), ((), ())), preferred_element_type=jnp.float32
    )
    vv = lax.psum_scatter(vv, "virt", scatter_dimension=0, tiled=True)
    low = lax.psum(vv, "pair").astype(jnp.bfloat16)
    blocks = lax.all_gather(jnp.transpose(chol_ov, (1, 2, 0)), "virt", axis=1, tiled=True)
    density = jnp.einsum("ab,ibq->iaq", low, blocks, preferred_element_type=jnp.float32)
    return jnp.transpose(density, (2, 0, 1)).astype(jnp.bfloat16)


def solution(mesh):
    count, groups = mesh.shape["virt"], mesh.shape["pair"]
    paired = count & (count - 1) == 0 and groups & (groups - 1) == 0 and count > 3 and groups > 1

    def shards(lambda_amps, t2_amps, chol_ov):
        if paired and chol_ov.shape[2] % 16 == 0 and chol_ov.shape[1] > 1:
            return permuted(count, groups, lambda_amps, t2_amps, chol_ov)
        return gathered(lambda_amps, t2_amps, chol_ov)

    placed = (P("pair", "virt", None), P("pair", "virt", None), P("pair", None, "virt"))
    return jax.shard_map(
        shards, mesh=mesh, in_specs=placed, out_specs=P("pair", None, "virt"), check_vma=False
    )
```
